1024 devices in a mesh: dp: 128 (over z, y), fsdp: 8 (over x, core).
Axes of the slice: x: 4, y: 4, z: 32, core: 2. Of those that a mesh axis runs over, the one named last changes fastest.
Arguments:
- queries: bfloat16 [32768, 3072], P('dp', 'fsdp'), may hold values from -1.4 to 1.4
- key_rows: bfloat16 [32768, 3072], P('dp', 'fsdp'), may hold values from -5 to 5
- values: bfloat16 [32768, 3072], P('dp', 'fsdp'), may hold values from -20 to 20
- log_decay: float32 [32, 32768], P('fsdp', 'dp'), may hold values from -0.8 to 0
- segment_ids: int32 [32768], P('dp'), may hold values from 0 to 63, as said below
- norm_gain: float32 [3072], P('fsdp'), may hold values from 0.5 to 1.5
- grad_out: bfloat16 [32768, 3072], P('dp', 'fsdp'), may hold values from -8 to 8
Outputs:
- attended: bfloat16 [32768, 3072], P('dp', 'fsdp')
- grad_queries: bfloat16 [32768, 3072], P('dp', 'fsdp')
- grad_keys: bfloat16 [32768, 3072], P('dp', 'fsdp')
- grad_values: bfloat16 [32768, 3072], P('dp', 'fsdp')
- grad_gain: float32 [3072], P('fsdp')
The draws below stay inside these ranges and needn't reach their ends.
Inputs may be any that keep to these rules, and one draw needn't show every extreme that they name: `segment_ids`: each response is one run of consecutive packed tokens; the ids rise by one from response to response and every id is used; every response's length is a multiple of 128 and at most 16384; one response has exactly 16384 tokens.
All inputs are finite; a program needn't handle non-finite values.
Results may differ from the reference program's by a relative error of at most 0.0056.
Values sent between devices are 32-bit elements; how exact they have to be, the bound alone decides.
No kernel may reach another device: no remote copies, remote signals or barrier semaphores. Data moves between devices by JAX's collectives and lax.ppermute only.
A program may use at most 128 MiB of HBM per device.

```python
import jax
import jax.numpy as jnp
from jax import lax

HD = 96
SHARD_ATTN_COUNT = 32
BLOCK = 256
TOK_DEV = 256
CONCAT_POSITIONS = 32768
SEQS = 64
MAX_REPLY_SPAN = 16384


def draw_queries(key, part):
    key = jax.random.fold_in(key, 11)
    stochastic_partition = jax.random.split(key, 2)
    base_draw = jnp.clip(jax.random.normal(stochastic_partition[0], (CONCAT_POSITIONS, SHARD_ATTN_COUNT * HD)), -4.0, 4.0)
    row_scale = jnp.exp(jax.random.uniform(stochastic_partition[1], (CONCAT_POSITIONS, 1), minval=jnp.log(0.3), maxval=jnp.log(3.0)))
    return jnp.clip(base_draw * row_scale * HD ** (-0.5), -1.4, 1.4).astype(jnp.bfloat16)


def draw_values(key, part):
    key = jax.random.fold_in(key, 23)
    stochastic_partition = jax.random.split(key, 2)
    channel = jnp.exp(jax.random.uniform(stochastic_partition[1], (1, SHARD_ATTN_COUNT * HD), minval=jnp.log(0.3), maxval=jnp.log(3.0)))
    head_index = (jnp.arange(SHARD_ATTN_COUNT * HD) // HD).astype(jnp.float32)
    rising = 0.6 * 3.0 ** (head_index / max(SHARD_ATTN_COUNT - 1, 1))
    base_draw = jnp.clip(jax.random.normal(stochastic_partition[0], (CONCAT_POSITIONS, SHARD_ATTN_COUNT * HD)), -4.0, 4.0)
    return jnp.clip(base_draw * channel * rising[None, :], -20.0, 20.0).astype(jnp.bfloat16)


def draw_grad_out(key, part):
    key = jax.random.fold_in(key, 37)
    stochastic_partition = jax.random.split(key, 1)
    fraction = jnp.arange(CONCAT_POSITIONS).astype(jnp.float32)[:, None] / CONCAT_POSITIONS
    base_draw = jnp.clip(jax.random.normal(stochastic_partition[0], (CONCAT_POSITIONS, SHARD_ATTN_COUNT * HD)), -4.0, 4.0)
    profile = 0.6 + 1.2 * fraction
    return jnp.clip(base_draw * profile, -8.0, 8.0).astype(jnp.bfloat16)


def draw_log_decay(key, part):
    key = jax.random.fold_in(key, 7)
    stochastic_partition = jax.random.split(key, 7)
    fast_share = 0.5
    chooser = jax.random.uniform(stochastic_partition[0], (SHARD_ATTN_COUNT, 1))
    fast_rate = jnp.exp(jax.random.uniform(stochastic_partition[1], (SHARD_ATTN_COUNT, 1), minval=jnp.log(1.0 / 50.0), maxval=jnp.log(1.0 / 30.0)))
    slow_rate = jnp.exp(jax.random.uniform(stochastic_partition[2], (SHARD_ATTN_COUNT, 1), minval=jnp.log(0.03), maxval=jnp.log(0.3))) / MAX_REPLY_SPAN
    nominal_speed = jnp.where(chooser < fast_share, fast_rate, slow_rate)
    worker_speed_factor = jnp.exp(jax.random.uniform(stochastic_partition[3], (SHARD_ATTN_COUNT, CONCAT_POSITIONS // TOK_DEV), minval=jnp.log(0.6), maxval=jnp.log(1.5)))
    worker_speed_factor = jnp.repeat(worker_speed_factor, TOK_DEV, axis=1)
    unevenness = jax.random.uniform(stochastic_partition[4], (SHARD_ATTN_COUNT, CONCAT_POSITIONS), minval=0.7, maxval=1.3)
    spike_switch = jax.random.bernoulli(stochastic_partition[5], 2.0 / MAX_REPLY_SPAN, (SHARD_ATTN_COUNT, CONCAT_POSITIONS))
    spike_duration = jnp.log(jax.random.uniform(stochastic_partition[6], (SHARD_ATTN_COUNT, CONCAT_POSITIONS), minval=0.5, maxval=0.8))
    closing_result = -nominal_speed * worker_speed_factor * unevenness + jnp.where(spike_switch, spike_duration, 0.0)
    return jnp.clip(closing_result, -0.8, 0.0).astype(jnp.float32)


def draw_segment_ids(key, part):
    key = jax.random.fold_in(key, 41)
    stochastic_partition = jax.random.split(key, 2)
    unit_span = BLOCK // 2
    units_all = CONCAT_POSITIONS // unit_span
    most_units = MAX_REPLY_SPAN // unit_span
    rest_units = units_all - most_units
    cut_place = jnp.arange(1, rest_units).astype(jnp.int32)
    noise = jax.random.randint(stochastic_partition[0], (rest_units - 1,), 0, 65536, dtype=jnp.int32)
    forced = cut_place % most_units == 0
    score = jnp.where(forced, jnp.int32(2 ** 30) + cut_place, noise * rest_units + cut_place).astype(jnp.int32)
    chosen_scores, chosen_places = lax.top_k(score, SEQS - 2)
    threshold = chosen_scores[SEQS - 3]
    is_cut = (score >= threshold).astype(jnp.int32)
    other_id = jnp.concatenate([jnp.zeros((1,), jnp.int32), jnp.cumsum(is_cut).astype(jnp.int32)])
    slot = jax.random.randint(stochastic_partition[1], (), 0, SEQS, dtype=jnp.int32)
    start_long = jnp.sum((other_id < slot).astype(jnp.int32)).astype(jnp.int32)
    position = jnp.arange(units_all).astype(jnp.int32)
    drawn_id = other_id[jnp.clip(position, 0, rest_units - 1)]
    shifted_id = other_id[jnp.clip(position - most_units, 0, rest_units - 1)] + 1
    unit_id = jnp.where(position < start_long, drawn_id, jnp.where(position < start_long + most_units, slot, shifted_id))
    return jnp.repeat(unit_id, unit_span).astype(jnp.int32)


def steps_of(stream_key, shape, pieces, low, top_value):
    loudness = 1.0
    for axis_at, blocks in pieces:
        steps = jax.random.uniform(jax.random.fold_in(jax.random.fold_in(stream_key, 6), axis_at), (blocks,), jnp.float32, low / len(pieces), top_value / len(pieces))
        loudness = loudness * jnp.repeat(jnp.exp(steps), shape[axis_at] // blocks).reshape((-1,) + (1,) * (len(shape) - 1 - axis_at))
    return loudness


def bell_draw(own_key, dims, scale, reach, cuts=(), held_as=jnp.bfloat16):
    result = jax.random.normal(own_key, dims, jnp.float32) * scale
    if len(cuts) > 0:
        result = steps_of(own_key, dims, cuts, -0.22, 0.18) * result
    return jnp.clip(result, min=-reach, max=reach).astype(held_as)


def setup_inputs(seed: int = 0) -> dict:
    arg_keys = jax.random.split(jax.random.key(seed), 8)
    queries = draw_queries(jax.random.fold_in(arg_keys[7], 71), 0)
    key_rows = bell_draw(arg_keys[1], (CONCAT_POSITIONS, SHARD_ATTN_COUNT * HD), 1.0, 5.0, ((0, 128), (1, 8)))
    values = draw_values(jax.random.fold_in(arg_keys[7], 71), 0)
    log_decay = draw_log_decay(jax.random.fold_in(arg_keys[7], 71), 0)
    segment_ids = draw_segment_ids(jax.random.fold_in(arg_keys[7], 71), 0)
    norm_gain = jnp.clip(1.0 + 0.1 * jax.random.normal(arg_keys[5], (SHARD_ATTN_COUNT * HD,), jnp.float32), 0.5, 1.5)
    grad_out = draw_grad_out(jax.random.fold_in(arg_keys[7], 71), 0)
    return dict(queries=queries, key_rows=key_rows, values=values, log_decay=log_decay, segment_ids=segment_ids, norm_gain=norm_gain, grad_out=grad_out)


EPSILON = 1e-06
PRECISE = lax.Precision.HIGHEST

def block_decays(decay_rows, segment_rows, blocks, width):
    head_count = decay_rows.shape[0]
    cumulative = jnp.cumsum(decay_rows.reshape(head_count, blocks, width), axis=2)
    segment_blk = segment_rows.reshape(blocks, width)
    first_seg = segment_blk[:, 0]
    last_seg = segment_blk[:, -1]
    causal = lax.broadcasted_iota(jnp.int32, (width, width), 0) >= lax.broadcasted_iota(jnp.int32, (width, width), 1)
    allowed = jnp.logical_and(segment_blk[:, :, None] == segment_blk[:, None, :], causal[None])[None]
    gap_decay = cumulative[:, :, :, None] - cumulative[:, :, None, :]
    decay_mask = jnp.where(allowed, jnp.exp(jnp.where(allowed, gap_decay, 0.0)), 0.0)
    lead_decay = jnp.exp(cumulative) * (segment_blk == first_seg[:, None])[None].astype(jnp.float32)
    tail_decay = jnp.exp(cumulative[:, :, -1:] - cumulative) * (segment_blk == last_seg[:, None])[None].astype(jnp.float32)
    through = jnp.exp(cumulative[:, :, -1]) * (first_seg == last_seg)[None].astype(jnp.float32)
    return (decay_mask, lead_decay, tail_decay, through, first_seg + 1, last_seg + 1)

def single_block(decay_one, segment_one):
    decay_mask, lead_decay, tail_decay, through, near_tag, far_tag = block_decays(decay_one, segment_one, 1, BLOCK)
    return (decay_mask[:, 0], lead_decay[:, 0], tail_decay[:, 0], through[:, 0], near_tag[0], far_tag[0])

def reference(queries, key_rows, values, log_decay, segment_ids, norm_gain, grad_out):
    blocks = CONCAT_POSITIONS // BLOCK
    query_b = queries.reshape(blocks, BLOCK, SHARD_ATTN_COUNT, HD)
    key_b = key_rows.reshape(blocks, BLOCK, SHARD_ATTN_COUNT, HD)
    value_b = values.reshape(blocks, BLOCK, SHARD_ATTN_COUNT, HD)
    decay_b = log_decay.reshape(SHARD_ATTN_COUNT, blocks, BLOCK).transpose(1, 0, 2)
    segment_b = segment_ids.reshape(blocks, BLOCK)

    def forward_step(carry, inputs):
        carried, carried_tag = carry
        query_one, key_one, value_one, decay_one, segment_one = inputs
        decay_mask, lead_decay, tail_decay, through, near_tag, far_tag = single_block(decay_one, segment_one)
        scores = jnp.einsum('thd,shd->hts', query_one.astype(jnp.float32), key_one.astype(jnp.float32), precision=PRECISE)
        attn_probs = (scores * decay_mask).astype(jnp.bfloat16)
        inner_part = jnp.einsum('hts,shd->thd', attn_probs.astype(jnp.float32), value_one.astype(jnp.float32), precision=PRECISE)
        joined = (carried_tag == near_tag).astype(jnp.float32)
        enter = lead_decay * joined
        outer_part = jnp.einsum('thd,hde->the', query_one.astype(jnp.float32), carried, precision=PRECISE)
        attention = inner_part + outer_part * enter.T[:, :, None]
        keyed = (key_one.astype(jnp.float32) * tail_decay.T[:, :, None]).astype(jnp.bfloat16)
        summary = jnp.einsum('shd,she->hde', keyed.astype(jnp.float32), value_one.astype(jnp.float32), precision=PRECISE)
        updated = summary + (through * joined)[:, None, None] * carried
        return ((updated, far_tag), (attention, carried, carried_tag))
    start = (jnp.zeros((SHARD_ATTN_COUNT, HD, HD), jnp.float32), jnp.zeros((), jnp.int32))
    ignored, (attention, states_in, tags_in) = lax.scan(forward_step, start, (query_b, key_b, value_b, decay_b, segment_b))
    attention = attention.reshape(CONCAT_POSITIONS, SHARD_ATTN_COUNT * HD)
    squares = lax.optimization_barrier(jnp.sum(attention * attention, axis=1))
    inv_rms = lax.rsqrt(squares / (SHARD_ATTN_COUNT * HD) + EPSILON)
    normed = attention * inv_rms[:, None]
    attended = (normed * norm_gain[None, :]).astype(jnp.bfloat16)
    grad_float = grad_out.astype(jnp.float32)
    grad_normed = grad_float * norm_gain[None, :]
    dot_terms = lax.optimization_barrier(jnp.sum(grad_normed * normed, axis=1))
    grad_attn = (inv_rms[:, None] * (grad_normed - normed * (dot_terms / (SHARD_ATTN_COUNT * HD))[:, None])).astype(jnp.bfloat16)
    grad_gain = lax.optimization_barrier(jnp.sum(grad_float * normed, axis=0)) * CONCAT_POSITIONS ** (-0.5)
    grad_b = grad_attn.reshape(blocks, BLOCK, SHARD_ATTN_COUNT, HD)

    def backward_step(carry, inputs):
        carried, carried_tag = carry
        query_one, key_one, value_one, grad_one, decay_one, segment_one, state_in, tag_in = inputs
        decay_mask, lead_decay, tail_decay, through, near_tag, far_tag = single_block(decay_one, segment_one)
        query_f = query_one.astype(jnp.float32)
        key_f = key_one.astype(jnp.float32)
        value_f = value_one.astype(jnp.float32)
        grad_f = grad_one.astype(jnp.float32)
        scores = jnp.einsum('thd,shd->hts', query_f, key_f, precision=PRECISE)
        attn_probs = (scores * decay_mask).astype(jnp.bfloat16)
        enter = lead_decay * (tag_in == near_tag).astype(jnp.float32)
        score_grads = (jnp.einsum('thd,shd->hts', grad_f, value_f, precision=PRECISE) * decay_mask).astype(jnp.bfloat16)
        grad_query = jnp.einsum('hts,shd->thd', score_grads.astype(jnp.float32), key_f, precision=PRECISE)
        grad_query = grad_query + jnp.einsum('the,hde->thd', grad_f, state_in, precision=PRECISE) * enter.T[:, :, None]
        joined = (carried_tag == far_tag).astype(jnp.float32)
        leave = (tail_decay * joined).T[:, :, None]
        grad_key = jnp.einsum('hts,thd->shd', score_grads.astype(jnp.float32), query_f, precision=PRECISE)
        grad_key = grad_key + jnp.einsum('hde,she->shd', carried, value_f, precision=PRECISE) * leave
        grad_value = jnp.einsum('hts,thd->shd', attn_probs.astype(jnp.float32), grad_f, precision=PRECISE)
        grad_value = grad_value + jnp.einsum('shd,hde->she', key_f, carried, precision=PRECISE) * leave
        queued = (query_f * lead_decay.T[:, :, None]).astype(jnp.bfloat16)
        summary = jnp.einsum('thd,the->hde', queued.astype(jnp.float32), grad_f, precision=PRECISE)
        updated = summary + (through * joined)[:, None, None] * carried
        return ((updated, near_tag), (grad_query, grad_key, grad_value))
    ignored, (grad_q, grad_k, grad_v) = lax.scan(backward_step, start, (query_b, key_b, value_b, grad_b, decay_b, segment_b, states_in, tags_in), reverse=True)
    grad_queries = grad_q.reshape(CONCAT_POSITIONS, SHARD_ATTN_COUNT * HD).astype(jnp.bfloat16)
    grad_keys = grad_k.reshape(CONCAT_POSITIONS, SHARD_ATTN_COUNT * HD).astype(jnp.bfloat16)
    grad_values = grad_v.reshape(CONCAT_POSITIONS, SHARD_ATTN_COUNT * HD).astype(jnp.bfloat16)
    return (attended, grad_queries, grad_keys, grad_values, grad_gain)
```

```python
import functools

import jax
import jax.numpy as jnp
from jax import lax
from jax.experimental import pallas as pl
from jax.experimental.pallas import tpu as pltpu
from jax.sharding import Mesh
from jax.sharding import PartitionSpec as P

BLOCK = 256
EPSILON = 1e-06
PRECISE = lax.Precision.HIGHEST
PASS, NEAR, FAR, GAIN = 96, 97, 98, 99


def links(near, far):
    return [None] + [(far[k - 1] == near[k]).astype(jnp.float32) for k in range(1, len(near))]


def columns(ref, count):
    picked = [[ref[k, :, lane : lane + 1] for k in range(count)] for lane in (PASS, NEAR, FAR)]
    return picked


def total_kernel(backward, pieces_ref, out_ref):
    count, rows, lanes = pieces_ref.shape
    order = list(range(count))[::-1] if backward else list(range(count))
    passes, near, far = columns(pieces_ref, count)
    if backward:
        near, far = far, near
    lane = lax.broadcasted_iota(jnp.int32, (rows, lanes), 1)
    running = pieces_ref[order[0]]
    gain = running
    through = passes[order[0]]
    for before, k in zip(order[:-1], order[1:]):
        piece = pieces_ref[k]
        carried = passes[k] * (far[before] == near[k]).astype(jnp.float32)
        running = piece + carried * running
        through = through * carried
        gain = gain + piece
    first, last = order[0], order[-1]
    out = jnp.where(lane < PASS, running, gain)
    out = jnp.where(lane == PASS, through, out)
    out = jnp.where(lane == NEAR, near[first], out)
    out = jnp.where(lane == FAR, far[last], out)
    for g in range(out_ref.shape[0]):
        out_ref[g] = out


def prefix_kernel(backward, mine_ref, pieces_ref, groups_ref, out_ref):
    count, rows, lanes = pieces_ref.shape
    group_count = groups_ref.shape[0]
    mine = mine_ref[0]
    lane = lax.broadcasted_iota(jnp.int32, (rows, lanes), 1)
    group_order = list(range(group_count))[::-1] if backward else list(range(group_count))
    running = jnp.zeros((rows, lanes), jnp.float32)
    gain = jnp.zeros((rows, lanes), jnp.float32)
    last_far = jnp.full((rows, 1), -1.0, jnp.float32)
    entering = running
    entering_far = last_far
    for g in group_order:
        here = mine == g
        entering = jnp.where(here, running, entering)
        entering_far = jnp.where(here, last_far, entering_far)
        piece = groups_ref[g]
        joined = (last_far == piece[:, NEAR : NEAR + 1]).astype(jnp.float32)
        running = piece + (piece[:, PASS : PASS + 1] * joined) * running
        gain = gain + piece
        last_far = piece[:, FAR : FAR + 1]
    order = list(range(count))[::-1] if backward else list(range(count))
    passes, near, far = columns(pieces_ref, count)
    if backward:
        near, far = far, near
    state = entering
    before_far = entering_far
    for k in order:
        joined = (before_far == near[k]).astype(jnp.float32)
        state = state * joined
        out_ref[k] = jnp.where(lane < PASS, state, gain)
        state = pieces_ref[k] + passes[k] * state
        before_far = far[k]


def scan_states(summary, through, near, far, gain, backward):
    head_count, rows, cols = summary.shape
    group = lax.axis_size("near")
    parts = group // head_count
    sub = rows // parts
    extra = jnp.stack(
        [
            jnp.broadcast_to(through[:, None], (head_count, rows)),
            jnp.broadcast_to(near.astype(jnp.float32), (head_count, rows)),
            jnp.broadcast_to(far.astype(jnp.float32), (head_count, rows)),
            gain,
        ],
        axis=2,
    )
    extra = jnp.pad(extra, ((0, 0), (0, 0), (0, 128 - cols - 4)))
    pieces = jnp.concatenate([summary, extra], axis=2).reshape(group, sub, 128)
    pieces = lax.all_to_all(pieces, "near", 0, 0, tiled=True)
    group_count = lax.axis_size("wide")
    total = pl.pallas_call(
        functools.partial(total_kernel, backward),
        out_shape=jax.ShapeDtypeStruct((group_count, sub, 128), jnp.float32),
        name="group_total",
    )(pieces)
    groups = lax.all_to_all(total, "wide", 0, 0, tiled=True)
    mine = lax.axis_index("wide").astype(jnp.int32).reshape(1)
    states = pl.pallas_call(
        functools.partial(prefix_kernel, backward),
        out_shape=jax.ShapeDtypeStruct((group, sub, 128), jnp.float32),
        in_specs=[
            pl.BlockSpec(memory_space=pltpu.SMEM),
            pl.BlockSpec(memory_space=pltpu.VMEM),
            pl.BlockSpec(memory_space=pltpu.VMEM),
        ],
        name="group_prefix",
    )(mine, pieces, groups)
    states = lax.all_to_all(states, "near", 0, 0, tiled=True).reshape(head_count, rows, 128)
    return states[:, :, :cols], states[:, :, GAIN]


def local(queries, key_rows, values, log_decay, segment_ids, norm_gain, grad_out):
    row_count, feature_count = queries.shape
    head_count = log_decay.shape[0]
    head_size = feature_count // head_count
    dp_count = lax.axis_size("wide") * lax.axis_size("near")
    query_b = queries.reshape(row_count, head_count, head_size)
    key_b = key_rows.reshape(row_count, head_count, head_size)
    value_b = values.reshape(row_count, head_count, head_size)
    cumulative = jnp.cumsum(log_decay, axis=1)
    near, far = segment_ids[0], segment_ids[-1]
    causal = lax.broadcasted_iota(jnp.int32, (BLOCK, BLOCK), 0) >= lax.broadcasted_iota(
        jnp.int32, (BLOCK, BLOCK), 1
    )
    allowed = jnp.logical_and(segment_ids[:, None] == segment_ids[None, :], causal)[None]
    gap = cumulative[:, :, None] - cumulative[:, None, :]
    decay_mask = jnp.where(allowed, jnp.exp(jnp.where(allowed, gap, 0.0)), 0.0)
    lead = jnp.exp(cumulative) * (segment_ids == near)[None].astype(jnp.float32)
    tail = jnp.exp(cumulative[:, -1:] - cumulative) * (segment_ids == far)[None].astype(jnp.float32)
    through = jnp.exp(cumulative[:, -1]) * (near == far).astype(jnp.float32)
    lead = lead.T[..., None]
    tail = tail.T[..., None]
    keyed = (key_b * tail).astype(jnp.bfloat16)
    summary = jnp.einsum("shd,she->hde", keyed, value_b, preferred_element_type=jnp.float32)
    zeros = jnp.zeros((head_count, head_size), jnp.float32)
    state_in, _ = scan_states(summary, through, near, far, zeros, False)
    scores = jnp.einsum("thd,shd->hts", query_b, key_b, preferred_element_type=jnp.float32)
    attn_probs = (scores * decay_mask).astype(jnp.bfloat16)
    inner = jnp.einsum("hts,shd->thd", attn_probs, value_b, preferred_element_type=jnp.float32)
    outer = jnp.einsum("thd,hde->the", query_b.astype(jnp.float32), state_in, precision=PRECISE)
    attention = (inner + outer * lead).reshape(row_count, feature_count)
    grad_float = grad_out.astype(jnp.float32)
    grad_normed = grad_float * norm_gain[None, :]
    sums = jnp.stack(
        [jnp.sum(attention * attention, axis=1), jnp.sum(grad_normed * attention, axis=1)]
    )
    fsdp = lax.axis_size("fsdp")
    sums = lax.all_to_all(
        jnp.broadcast_to(sums[None], (fsdp, 2, row_count)), "fsdp", 0, 0, tiled=True
    ).sum(axis=0)
    width = feature_count * fsdp
    inv_rms = lax.rsqrt(sums[0] / width + EPSILON)
    dots = sums[1] * inv_rms / width
    normed = attention * inv_rms[:, None]
    attended = (normed * norm_gain[None, :]).astype(jnp.bfloat16)
    grad_attn = (inv_rms[:, None] * (grad_normed - normed * dots[:, None])).astype(jnp.bfloat16)
    gain_terms = jnp.sum(grad_float * normed, axis=0).reshape(head_count, head_size)
    grad_b = grad_attn.reshape(row_count, head_count, head_size)
    queued = (query_b * lead).astype(jnp.bfloat16)
    back_summary = jnp.einsum("thd,the->hde", queued, grad_b, preferred_element_type=jnp.float32)
    back_in, gain = scan_states(back_summary, through, near, far, gain_terms, True)
    grad_gain = gain.reshape(feature_count) * float(row_count * dp_count) ** (-0.5)
    score_grads = (
        jnp.einsum("thd,shd->hts", grad_b, value_b, preferred_element_type=jnp.float32) * decay_mask
    ).astype(jnp.bfloat16)
    grad_q = jnp.einsum("hts,shd->thd", score_grads, key_b, preferred_element_type=jnp.float32)
    grad_q = (
        grad_q
        + jnp.einsum("the,hde->thd", grad_b.astype(jnp.float32), state_in, precision=PRECISE) * lead
    )
    grad_k = jnp.einsum("hts,thd->shd", score_grads, query_b, preferred_element_type=jnp.float32)
    grad_v = jnp.einsum("hts,thd->shd", attn_probs, grad_b, preferred_element_type=jnp.float32)
    grad_k = (
        grad_k
        + jnp.einsum("hde,she->shd", back_in, value_b.astype(jnp.float32), precision=PRECISE) * tail
    )
    grad_v = (
        grad_v
        + jnp.einsum("shd,hde->she", key_b.astype(jnp.float32), back_in, precision=PRECISE) * tail
    )
    shape = (row_count, feature_count)
    return (
        attended,
        grad_q.reshape(shape).astype(jnp.bfloat16),
        grad_k.reshape(shape).astype(jnp.bfloat16),
        grad_v.reshape(shape).astype(jnp.bfloat16),
        grad_gain,
    )


def solution(mesh):
    dp_count, fsdp_count = mesh.devices.shape
    near_count = 16
    fine = Mesh(
        mesh.devices.reshape(dp_count // near_count, near_count, fsdp_count),
        ("wide", "near", "fsdp"),
    )
    dp = ("wide", "near")
    return jax.shard_map(
        local,
        mesh=fine,
        in_specs=(
            P(dp, "fsdp"),
            P(dp, "fsdp"),
            P(dp, "fsdp"),
            P("fsdp", dp),
            P(dp),
            P("fsdp"),
            P(dp, "fsdp"),
        ),
        out_specs=(P(dp, "fsdp"), P(dp, "fsdp"), P(dp, "fsdp"), P(dp, "fsdp"), P("fsdp")),
        check_vma=False,
    )
```

```python
import functools

import jax
import jax.numpy as jnp
from jax import lax
from jax.experimental import pallas as pl
from jax.experimental.pallas import tpu as pltpu
from jax.sharding import Mesh
from jax.sharding import PartitionSpec as P

BLOCK = 256
EPSILON = 1e-06
PRECISE = lax.Precision.HIGHEST
PASS, NEAR, FAR, GAIN = 96, 97, 98, 99


HEADS, HEAD, TILE = 4, 96, 128
SUB = 24
STARTS = tuple(HEAD * h % TILE for h in range(HEADS))
WINDOWS = tuple((HEAD * h // TILE, (HEAD * h + HEAD - 1) // TILE + 1) for h in range(HEADS))


def on_chip(kernel, outs, operands, name, flops=0, exps=0):
    placed, specs, moved = [], [], 0
    for x in operands:
        if x.dtype == jnp.int32:
            placed.append(x)
            specs.append(pl.BlockSpec(memory_space=pltpu.SMEM))
        else:
            placed.append(pltpu.with_memory_space_constraint(x, pltpu.VMEM))
            specs.append(pl.BlockSpec(memory_space=pltpu.VMEM))
            moved += x.size * x.dtype.itemsize
    for out in outs:
        moved += out.size * out.dtype.itemsize if hasattr(out, "size") else 0
    return pl.pallas_call(
        kernel,
        out_shape=outs,
        in_specs=specs,
        out_specs=[pl.BlockSpec(memory_space=pltpu.VMEM) for _ in outs],
        cost_estimate=pl.CostEstimate(
            flops=flops, bytes_accessed=moved, transcendentals=exps
        ),
        compiler_params=pltpu.CompilerParams(vmem_limit_bytes=40 * 1024 * 1024),
        name=name,
    )(*placed)


def dot(a, b, over_a=1, over_b=0):
    return lax.dot_general(
        a, b, (((over_a,), (over_b,)), ((), ())), preferred_element_type=jnp.float32
    )


def pick_heads(parts, tile, rows):
    lane = lax.broadcasted_iota(jnp.int32, (rows, TILE), 1) + tile * TILE
    inside = [h for h in range(HEADS) if WINDOWS[h][0] <= tile < WINDOWS[h][1]]
    out = parts[inside[-1]]
    for h in inside[:-1][::-1]:
        out = jnp.where(lane < HEAD * (h + 1), parts[h], out)
    return out


def over_features(cols, first, rows):
    spread = [jnp.broadcast_to(cols[:, first + h : first + h + 1], (rows, TILE)) for h in range(HEADS)]
    return jnp.concatenate([pick_heads(spread, c, rows) for c in range(3)], axis=1)


def only_head(x, h):
    low, high = WINDOWS[h]
    x = x[:, low * TILE : high * TILE]
    lane = lax.broadcasted_iota(jnp.int32, x.shape, 1) + low * TILE
    inside = jnp.logical_and(lane >= HEAD * h, lane < HEAD * (h + 1))
    return jnp.where(inside, x, jnp.zeros_like(x))


def write_pieces(left, right, rows_ref, gain, out_ref):
    full = dot(left, right, 0, 0)
    lane = lax.broadcasted_iota(jnp.int32, (HEAD, TILE), 1)
    last = BLOCK - 1
    same, near, far = (rows_ref[r : r + 1, last:] for r in (4, 5, 6))
    for h in range(HEADS):
        low, high = WINDOWS[h]
        tiles = [full[HEAD * h : HEAD * (h + 1), TILE * c : TILE * (c + 1)] for c in range(low, high)]
        state = tiles[0] if len(tiles) == 1 else jnp.where(lane >= STARTS[h], tiles[0], tiles[1])
        if STARTS[h]:
            state = pltpu.roll(state, TILE - STARTS[h], 1)
        through = jnp.exp(rows_ref[h : h + 1, last:]) * same
        state = jnp.where(lane < HEAD, state, through)
        state = jnp.where(lane == NEAR, near, state)
        state = jnp.where(lane == FAR, far, state)
        state = jnp.where(lane == GAIN, 0.0 if gain is None else gain[HEAD * h : HEAD * (h + 1)], state)
        for i in range(HEAD // SUB):
            out_ref[h * (HEAD // SUB) + i] = state[i * SUB : (i + 1) * SUB]


def read_states(pieces_ref):
    lane = lax.broadcasted_iota(jnp.int32, (HEAD, TILE), 1)
    zero = jnp.zeros((HEAD, TILE), jnp.float32)
    parts = HEAD // SUB
    bands = []
    for h in range(HEADS):
        state = jnp.concatenate([pieces_ref[h * parts + i] for i in range(parts)], axis=0)
        state = jnp.where(lane < HEAD, state, 0.0)
        if STARTS[h]:
            state = pltpu.roll(state, STARTS[h], 1)
        low, high = WINDOWS[h]
        tiles = [zero] * 3
        if high - low == 1:
            tiles[low] = state
        else:
            tiles[low] = jnp.where(lane >= STARTS[h], state, 0.0)
            tiles[low + 1] = jnp.where(lane >= STARTS[h], 0.0, state)
        bands.append(jnp.concatenate(tiles, axis=1))
    whole = jnp.concatenate(bands, axis=0)
    high = whole.astype(jnp.bfloat16)
    return high, (whole - high.astype(jnp.float32)).astype(jnp.bfloat16)


def summary_kernel(segment_ref, decay_ref, key_ref, value_ref, pieces_ref, rows_ref, cols_ref):
    near, far = segment_ref[0], segment_ref[BLOCK - 1]
    same = (near == far).astype(jnp.float32)
    earlier = lax.broadcasted_iota(jnp.int32, (BLOCK, BLOCK), 0) <= lax.broadcasted_iota(
        jnp.int32, (BLOCK, BLOCK), 1
    )
    decay = decay_ref[...]
    decay = jnp.concatenate([decay, decay], axis=0)
    cumulative = jnp.dot(
        decay, earlier.astype(jnp.float32), precision=PRECISE, preferred_element_type=jnp.float32
    )
    row = lax.broadcasted_iota(jnp.int32, (8, BLOCK), 0)
    first_half = lax.broadcasted_iota(jnp.int32, (8, BLOCK), 1) < BLOCK // 2
    last = cumulative[:, BLOCK - 1 :]
    in_near = jnp.where(first_half, 1.0, same)
    in_far = jnp.where(first_half, same, 1.0)
    decays = jnp.where(
        row < HEADS, jnp.exp(cumulative) * in_near, jnp.exp(last - cumulative) * in_far
    )
    tags = jnp.where(row == 4, same, jnp.where(row == 5, near.astype(jnp.float32), far.astype(jnp.float32)))
    rows_ref[...] = jnp.where(row < HEADS, cumulative, tags)
    cols = jnp.transpose(jnp.concatenate([decays, cumulative], axis=0))
    cols_ref[...] = cols
    keyed = key_ref[...].astype(jnp.float32) * over_features(cols, 4, BLOCK)
    write_pieces(keyed.astype(jnp.bfloat16), value_ref[...], rows_ref, None, pieces_ref)


def decay_masks(rows_ref, cols_ref):
    t = lax.broadcasted_iota(jnp.int32, (BLOCK, BLOCK), 0)
    s = lax.broadcasted_iota(jnp.int32, (BLOCK, BLOCK), 1)
    half = BLOCK // 2
    together = jnp.logical_or((t < half) == (s < half), rows_ref[4:5, :] > 0.5)
    allowed = jnp.logical_and(t >= s, together)
    for h in range(HEADS):
        gap = cols_ref[:, 8 + h : 9 + h] - rows_ref[h : h + 1, :]
        yield h, jnp.exp(jnp.where(allowed, gap, -1e30))


def times_heads(weights, x, over):
    tiles = []
    for c in range(3):
        column = x[:, c * TILE : (c + 1) * TILE]
        parts = [
            dot(weights[h], column, over, 0) if WINDOWS[h][0] <= c < WINDOWS[h][1] else None
            for h in range(HEADS)
        ]
        tiles.append(pick_heads(parts, c, BLOCK))
    return jnp.concatenate(tiles, axis=1)


def inside_kernel(rows_ref, cols_ref, query_ref, key_ref, value_ref, probs_ref, inner_ref):
    query, key = query_ref[...], key_ref[...]
    weights = []
    for h, mask in decay_masks(rows_ref, cols_ref):
        low, high = WINDOWS[h]
        scores = dot(only_head(query, h), key[:, low * TILE : high * TILE], 1, 1)
        weights.append((scores * mask).astype(jnp.bfloat16))
        probs_ref[h] = weights[h]
    inner_ref[...] = times_heads(weights, value_ref[...], 1)


def attention_kernel(
    states_ref, inner_ref, cols_ref, query_ref, grad_ref, gain_ref, attention_ref, sums_ref
):
    high, low = read_states(states_ref)
    query = query_ref[...]
    outer = dot(query, high) + dot(query, low)
    attention = inner_ref[...] + outer * over_features(cols_ref[...], 0, BLOCK)
    attention_ref[...] = attention
    squares = attention * attention
    products = grad_ref[...].astype(jnp.float32) * gain_ref[...] * attention
    sums = []
    for x in (squares, products):
        x = x[:, :TILE] + x[:, TILE : 2 * TILE] + x[:, 2 * TILE :]
        sums.append(jnp.sum(jnp.transpose(x), axis=0, keepdims=True))
    sums = jnp.concatenate(sums, axis=0)
    for k in range(sums_ref.shape[0]):
        sums_ref[k] = sums


def gradient_kernel(
    width, sums_ref, attention_ref, grad_ref, gain_ref, rows_ref, cols_ref, query_ref,
    grad_attn_ref, inv_ref, pieces_ref,
):
    sums = sums_ref[0]
    for k in range(1, sums_ref.shape[0]):
        sums = sums + sums_ref[k]
    inv = lax.rsqrt(sums[0:1] / width + EPSILON)
    dots = sums[1:2] * inv / width
    row = lax.broadcasted_iota(jnp.int32, (8, BLOCK), 0)
    both = jnp.transpose(jnp.where(row == 0, inv, dots))
    inv_ref[...] = both
    inv, dots = both[:, 0:1], both[:, 1:2]
    normed = attention_ref[...] * inv
    grad = grad_ref[...].astype(jnp.float32)
    grad_attn = (inv * (grad * gain_ref[...] - normed * dots)).astype(jnp.bfloat16)
    grad_attn_ref[...] = grad_attn
    gain = jnp.sum(grad * normed, axis=0, keepdims=True)
    gain = jnp.transpose(jnp.broadcast_to(gain, (8, gain.shape[1])))
    queued = query_ref[...].astype(jnp.float32) * over_features(cols_ref[...], 0, BLOCK)
    write_pieces(queued.astype(jnp.bfloat16), grad_attn, rows_ref, gain[:, 0:1], pieces_ref)


def inside_back_kernel(
    rows_ref, cols_ref, query_ref, key_ref, value_ref, probs_ref, grad_attn_ref, states_ref,
    attention_ref, inv_ref, gain_ref,
    grad_query_ref, part_key_ref, part_value_ref, attended_ref,
):
    grad_attn, value = grad_attn_ref[...], value_ref[...]
    weights = []
    for h, mask in decay_masks(rows_ref, cols_ref):
        low, high = WINDOWS[h]
        grads = dot(only_head(grad_attn, h), value[:, low * TILE : high * TILE], 1, 1)
        weights.append((grads * mask).astype(jnp.bfloat16))
    high, low = read_states(states_ref)
    outer = dot(grad_attn, high, 1, 1) + dot(grad_attn, low, 1, 1)
    grad_query = times_heads(weights, key_ref[...], 1) + outer * over_features(cols_ref[...], 0, BLOCK)
    grad_query_ref[...] = grad_query.astype(jnp.bfloat16)
    part_key_ref[...] = times_heads(weights, query_ref[...], 0)
    part_value_ref[...] = times_heads([probs_ref[h] for h in range(HEADS)], grad_attn, 0)
    attended = attention_ref[...] * inv_ref[:, 0:1] * gain_ref[...]
    attended_ref[...] = attended.astype(jnp.bfloat16)


def last_kernel(
    scale, states_ref, cols_ref, key_ref, value_ref, part_key_ref, part_value_ref,
    grad_key_ref, grad_value_ref, grad_gain_ref,
):
    high, low = read_states(states_ref)
    tail = over_features(cols_ref[...], 4, BLOCK)
    key, value = key_ref[...], value_ref[...]
    outer = dot(value, high, 1, 1) + dot(value, low, 1, 1)
    grad_key_ref[...] = (part_key_ref[...] + outer * tail).astype(jnp.bfloat16)
    outer = dot(key, high) + dot(key, low)
    grad_value_ref[...] = (part_value_ref[...] + outer * tail).astype(jnp.bfloat16)
    count = states_ref.shape[0]
    gain = jnp.concatenate([states_ref[k] for k in range(count)], axis=0)
    grad_gain_ref[...] = jnp.transpose(gain)[GAIN : GAIN + 1] * scale


def scan_states(pieces, backward):
    group, sub, lanes = pieces.shape
    pieces = lax.all_to_all(pieces, "near", 0, 0, tiled=True)
    group_count = lax.axis_size("wide")
    (total,) = on_chip(
        functools.partial(total_kernel, backward),
        [pltpu.VMEM((group_count, sub, lanes), jnp.float32)],
        [pieces],
        "group_total",
    )
    groups = lax.all_to_all(total, "wide", 0, 0, tiled=True)
    mine = lax.axis_index("wide").astype(jnp.int32).reshape(1)
    (states,) = on_chip(
        functools.partial(prefix_kernel, backward),
        [pltpu.VMEM((group, sub, lanes), jnp.float32)],
        [mine, pieces, groups],
        "group_prefix",
    )
    return lax.all_to_all(states, "near", 0, 0, tiled=True)


def local(queries, key_rows, values, log_decay, segment_ids, norm_gain, grad_out):
    tokens, features = queries.shape
    group = lax.axis_size("near")
    dp_count = lax.axis_size("wide") * group
    fsdp = lax.axis_size("fsdp")
    full = (tokens, features)
    mxu = 2 * tokens * tokens * HEAD * HEADS
    pieces, rows, cols = on_chip(
        summary_kernel,
        [
            pltpu.VMEM((group, SUB, TILE), jnp.float32),
            pltpu.VMEM((8, tokens), jnp.float32),
            pltpu.VMEM((tokens, 16), jnp.float32),
        ],
        [segment_ids, log_decay, key_rows, values],
        "summary",
        flops=mxu,
    )
    probs, inner = on_chip(
        inside_kernel,
        [pltpu.VMEM((HEADS, tokens, tokens), jnp.bfloat16), pltpu.VMEM(full, jnp.float32)],
        [rows, cols, queries, key_rows, values],
        "inside",
        flops=4 * mxu,
        exps=HEADS * tokens * tokens,
    )
    state_in = scan_states(pieces, False)
    gain_row = norm_gain.reshape(1, features)
    attention, sums = on_chip(
        attention_kernel,
        [pltpu.VMEM(full, jnp.float32), pltpu.VMEM((fsdp, 2, tokens), jnp.float32)],
        [state_in, inner, cols, queries, grad_out, gain_row],
        "attention",
        flops=2 * mxu,
    )
    sums = lax.all_to_all(sums, "fsdp", 0, 0, tiled=True)
    grad_attn, inv, back_pieces = on_chip(
        functools.partial(gradient_kernel, features * fsdp),
        [
            pltpu.VMEM(full, jnp.bfloat16),
            pltpu.VMEM((tokens, 8), jnp.float32),
            pltpu.VMEM((group, SUB, TILE), jnp.float32),
        ],
        [sums, attention, grad_out, gain_row, rows, cols, queries],
        "gradient",
        flops=mxu,
    )
    grad_queries, part_key, part_value, attended = on_chip(
        inside_back_kernel,
        [
            jax.ShapeDtypeStruct(full, jnp.bfloat16),
            pltpu.VMEM(full, jnp.float32),
            pltpu.VMEM(full, jnp.float32),
            jax.ShapeDtypeStruct(full, jnp.bfloat16),
        ],
        [rows, cols, queries, key_rows, values, probs, grad_attn, state_in, attention, inv, gain_row],
        "inside_back",
        flops=8 * mxu,
        exps=HEADS * tokens * tokens,
    )
    back_in = scan_states(back_pieces, True)
    grad_keys, grad_values, grad_gain = on_chip(
        functools.partial(last_kernel, float(tokens * dp_count) ** (-0.5)),
        [
            jax.ShapeDtypeStruct(full, jnp.bfloat16),
            jax.ShapeDtypeStruct(full, jnp.bfloat16),
            jax.ShapeDtypeStruct((1, features), jnp.float32),
        ],
        [back_in, cols, key_rows, values, part_key, part_value],
        "last",
        flops=4 * mxu,
    )
    return (attended, grad_queries, grad_keys, grad_values, grad_gain.reshape(features))


def columns(ref, count):
    picked = [[ref[k, :, lane : lane + 1] for k in range(count)] for lane in (PASS, NEAR, FAR)]
    return picked


def total_kernel(backward, pieces_ref, out_ref):
    count, rows, lanes = pieces_ref.shape
    order = list(range(count))[::-1] if backward else list(range(count))
    passes, near, far = columns(pieces_ref, count)
    if backward:
        near, far = far, near
    lane = lax.broadcasted_iota(jnp.int32, (rows, lanes), 1)
    running = pieces_ref[order[0]]
    gain = running
    through = passes[order[0]]
    for before, k in zip(order[:-1], order[1:]):
        piece = pieces_ref[k]
        carried = passes[k] * (far[before] == near[k]).astype(jnp.float32)
        running = piece + carried * running
        through = through * carried
        gain = gain + piece
    first, last = order[0], order[-1]
    out = jnp.where(lane < PASS, running, gain)
    out = jnp.where(lane == PASS, through, out)
    out = jnp.where(lane == NEAR, near[first], out)
    out = jnp.where(lane == FAR, far[last], out)
    for g in range(out_ref.shape[0]):
        out_ref[g] = out


def prefix_kernel(backward, mine_ref, pieces_ref, groups_ref, out_ref):
    count, rows, lanes = pieces_ref.shape
    group_count = groups_ref.shape[0]
    mine = mine_ref[0]
    lane = lax.broadcasted_iota(jnp.int32, (rows, lanes), 1)
    group_order = list(range(group_count))[::-1] if backward else list(range(group_count))
    running = jnp.zeros((rows, lanes), jnp.float32)
    gain = jnp.zeros((rows, lanes), jnp.float32)
    last_far = jnp.full((rows, 1), -1.0, jnp.float32)
    entering = running
    entering_far = last_far
    for g in group_order:
        here = mine == g
        entering = jnp.where(here, running, entering)
        entering_far = jnp.where(here, last_far, entering_far)
        piece = groups_ref[g]
        joined = (last_far == piece[:, NEAR : NEAR + 1]).astype(jnp.float32)
        running = piece + (piece[:, PASS : PASS + 1] * joined) * running
        gain = gain + piece
        last_far = piece[:, FAR : FAR + 1]
    order = list(range(count))[::-1] if backward else list(range(count))
    passes, near, far = columns(pieces_ref, count)
    if backward:
        near, far = far, near
    state = entering
    before_far = entering_far
    for k in order:
        joined = (before_far == near[k]).astype(jnp.float32)
        state = state * joined
        out_ref[k] = jnp.where(lane < PASS, state, gain)
        state = pieces_ref[k] + passes[k] * state
        before_far = far[k]


def solution(mesh):
    dp_count, fsdp_count = mesh.devices.shape
    near_count = 16
    fine = Mesh(
        mesh.devices.reshape(dp_count // near_count, near_count, fsdp_count),
        ("wide", "near", "fsdp"),
    )
    dp = ("wide", "near")
    return jax.shard_map(
        local,
        mesh=fine,
        in_specs=(
            P(dp, "fsdp"),
            P(dp, "fsdp"),
            P(dp, "fsdp"),
            P("fsdp", dp),
            P(dp),
            P("fsdp"),
            P(dp, "fsdp"),
        ),
        out_specs=(P(dp, "fsdp"), P(dp, "fsdp"), P(dp, "fsdp"), P(dp, "fsdp"), P("fsdp")),
        check_vma=False,
    )
```

```python
import functools

import jax
import jax.numpy as jnp
from jax import lax
from jax.experimental import pallas as pl
from jax.experimental.pallas import tpu as pltpu
from jax.sharding import Mesh
from jax.sharding import PartitionSpec as P

BLOCK = 256
EPSILON = 1e-06
PRECISE = lax.Precision.HIGHEST
PASS, NEAR, FAR, GAIN = 96, 97, 98, 99


HEADS, HEAD, TILE = 4, 96, 128
SUB = 24
STARTS = tuple(HEAD * h % TILE for h in range(HEADS))
WINDOWS = tuple((HEAD * h // TILE, (HEAD * h + HEAD - 1) // TILE + 1) for h in range(HEADS))


def on_chip(kernel, outs, operands, name, flops=0, exps=0, held_in=pltpu.VMEM):
    placed, specs, moved = [], [], 0
    for x in operands:
        placed.append(pltpu.with_memory_space_constraint(x, held_in))
        inside = pltpu.SMEM if x.dtype == jnp.int32 else pltpu.VMEM
        specs.append(pl.BlockSpec(memory_space=inside))
        moved += x.size * x.dtype.itemsize
    for out in outs:
        moved += out.size * out.dtype.itemsize if hasattr(out, "size") else 0
    return pl.pallas_call(
        kernel,
        out_shape=outs,
        in_specs=specs,
        out_specs=[pl.BlockSpec(memory_space=pltpu.VMEM) for _ in outs],
        cost_estimate=pl.CostEstimate(
            flops=flops, bytes_accessed=moved, transcendentals=exps
        ),
        compiler_params=pltpu.CompilerParams(vmem_limit_bytes=40 * 1024 * 1024),
        name=name,
    )(*placed)


def dot(a, b, over_a=1, over_b=0):
    return lax.dot_general(
        a, b, (((over_a,), (over_b,)), ((), ())), preferred_element_type=jnp.float32
    )


def pick_heads(parts, tile, rows):
    lane = lax.broadcasted_iota(jnp.int32, (rows, TILE), 1) + tile * TILE
    inside = [h for h in range(HEADS) if WINDOWS[h][0] <= tile < WINDOWS[h][1]]
    out = parts[inside[-1]]
    for h in inside[:-1][::-1]:
        out = jnp.where(lane < HEAD * (h + 1), parts[h], out)
    return out


def over_features(cols, first, rows):
    spread = [jnp.broadcast_to(cols[:, first + h : first + h + 1], (rows, TILE)) for h in range(HEADS)]
    return jnp.concatenate([pick_heads(spread, c, rows) for c in range(3)], axis=1)


def only_head(x, h):
    low, high = WINDOWS[h]
    x = x[:, low * TILE : high * TILE]
    lane = lax.broadcasted_iota(jnp.int32, x.shape, 1) + low * TILE
    inside = jnp.logical_and(lane >= HEAD * h, lane < HEAD * (h + 1))
    return jnp.where(inside, x, jnp.zeros_like(x))


def write_pieces(left, right, rows_ref, gain, out_ref):
    full = dot(left, right, 0, 0)
    lane = lax.broadcasted_iota(jnp.int32, (HEAD, TILE), 1)
    last = BLOCK - 1
    same, near, far = (rows_ref[r : r + 1, last:] for r in (4, 5, 6))
    for h in range(HEADS):
        low, high = WINDOWS[h]
        tiles = [full[HEAD * h : HEAD * (h + 1), TILE * c : TILE * (c + 1)] for c in range(low, high)]
        state = tiles[0] if len(tiles) == 1 else jnp.where(lane >= STARTS[h], tiles[0], tiles[1])
        if STARTS[h]:
            state = pltpu.roll(state, TILE - STARTS[h], 1)
        through = jnp.exp(rows_ref[h : h + 1, last:]) * same
        state = jnp.where(lane < HEAD, state, through)
        state = jnp.where(lane == NEAR, near, state)
        state = jnp.where(lane == FAR, far, state)
        state = jnp.where(lane == GAIN, 0.0 if gain is None else gain[HEAD * h : HEAD * (h + 1)], state)
        for i in range(HEAD // SUB):
            out_ref[h * (HEAD // SUB) + i] = state[i * SUB : (i + 1) * SUB]


def read_states(pieces_ref):
    lane = lax.broadcasted_iota(jnp.int32, (HEAD, TILE), 1)
    zero = jnp.zeros((HEAD, TILE), jnp.float32)
    parts = HEAD // SUB
    bands = []
    for h in range(HEADS):
        state = jnp.concatenate([pieces_ref[h * parts + i] for i in range(parts)], axis=0)
        state = jnp.where(lane < HEAD, state, 0.0)
        if STARTS[h]:
            state = pltpu.roll(state, STARTS[h], 1)
        low, high = WINDOWS[h]
        tiles = [zero] * 3
        if high - low == 1:
            tiles[low] = state
        else:
            tiles[low] = jnp.where(lane >= STARTS[h], state, 0.0)
            tiles[low + 1] = jnp.where(lane >= STARTS[h], 0.0, state)
        bands.append(jnp.concatenate(tiles, axis=1))
    whole = jnp.concatenate(bands, axis=0)
    high = whole.astype(jnp.bfloat16)
    return high, (whole - high.astype(jnp.float32)).astype(jnp.bfloat16)


def summary_kernel(segment_ref, decay_ref, key_ref, value_ref, pieces_ref, rows_ref, cols_ref):
    near, far = segment_ref[0], segment_ref[BLOCK - 1]
    same = (near == far).astype(jnp.float32)
    earlier = lax.broadcasted_iota(jnp.int32, (BLOCK, BLOCK), 0) <= lax.broadcasted_iota(
        jnp.int32, (BLOCK, BLOCK), 1
    )
    decay = decay_ref[...]
    decay = jnp.concatenate([decay, decay], axis=0)
    cumulative = jnp.dot(
        decay, earlier.astype(jnp.float32), precision=PRECISE, preferred_element_type=jnp.float32
    )
    row = lax.broadcasted_iota(jnp.int32, (8, BLOCK), 0)
    first_half = lax.broadcasted_iota(jnp.int32, (8, BLOCK), 1) < BLOCK // 2
    last = cumulative[:, BLOCK - 1 :]
    in_near = jnp.where(first_half, 1.0, same)
    in_far = jnp.where(first_half, same, 1.0)
    decays = jnp.where(
        row < HEADS, jnp.exp(cumulative) * in_near, jnp.exp(last - cumulative) * in_far
    )
    tags = jnp.where(row == 4, same, jnp.where(row == 5, near.astype(jnp.float32), far.astype(jnp.float32)))
    rows_ref[...] = jnp.where(row < HEADS, cumulative, tags)
    cols = jnp.transpose(jnp.concatenate([decays, cumulative], axis=0))
    cols_ref[...] = cols
    keyed = key_ref[...].astype(jnp.float32) * over_features(cols, 4, BLOCK)
    write_pieces(keyed.astype(jnp.bfloat16), value_ref[...], rows_ref, None, pieces_ref)


def decay_masks(rows_ref, cols_ref):
    t = lax.broadcasted_iota(jnp.int32, (BLOCK, BLOCK), 0)
    s = lax.broadcasted_iota(jnp.int32, (BLOCK, BLOCK), 1)
    half = BLOCK // 2
    together = jnp.logical_or((t < half) == (s < half), rows_ref[4:5, :] > 0.5)
    allowed = jnp.logical_and(t >= s, together)
    for h in range(HEADS):
        gap = cols_ref[:, 8 + h : 9 + h] - rows_ref[h : h + 1, :]
        yield h, jnp.exp(jnp.where(allowed, gap, -1e30))


def times_heads(weights, x, over):
    tiles = []
    for c in range(3):
        column = x[:, c * TILE : (c + 1) * TILE]
        parts = [
            dot(weights[h], column, over, 0) if WINDOWS[h][0] <= c < WINDOWS[h][1] else None
            for h in range(HEADS)
        ]
        tiles.append(pick_heads(parts, c, BLOCK))
    return jnp.concatenate(tiles, axis=1)


def inside_kernel(rows_ref, cols_ref, query_ref, key_ref, value_ref, probs_ref, inner_ref):
    query, key = query_ref[...], key_ref[...]
    weights = []
    for h, mask in decay_masks(rows_ref, cols_ref):
        low, high = WINDOWS[h]
        scores = dot(only_head(query, h), key[:, low * TILE : high * TILE], 1, 1)
        weights.append((scores * mask).astype(jnp.bfloat16))
        probs_ref[h] = weights[h]
    inner_ref[...] = times_heads(weights, value_ref[...], 1)


def attention_kernel(
    states_ref, inner_ref, cols_ref, query_ref, grad_ref, gain_ref, attention_ref, sums_ref
):
    high, low = read_states(states_ref)
    query = query_ref[...]
    outer = dot(query, high) + dot(query, low)
    attention = inner_ref[...] + outer * over_features(cols_ref[...], 0, BLOCK)
    attention_ref[...] = attention
    squares = attention * attention
    products = grad_ref[...].astype(jnp.float32) * gain_ref[...] * attention
    sums = []
    for x in (squares, products):
        x = x[:, :TILE] + x[:, TILE : 2 * TILE] + x[:, 2 * TILE :]
        sums.append(jnp.sum(jnp.transpose(x), axis=0, keepdims=True))
    sums = jnp.concatenate(sums, axis=0)
    for k in range(sums_ref.shape[0]):
        sums_ref[k] = sums


def gradient_kernel(
    width, sums_ref, attention_ref, grad_ref, gain_ref, rows_ref, cols_ref, query_ref,
    grad_attn_ref, inv_ref, pieces_ref,
):
    sums = sums_ref[0]
    for k in range(1, sums_ref.shape[0]):
        sums = sums + sums_ref[k]
    inv = lax.rsqrt(sums[0:1] / width + EPSILON)
    dots = sums[1:2] * inv / width
    row = lax.broadcasted_iota(jnp.int32, (8, BLOCK), 0)
    both = jnp.transpose(jnp.where(row == 0, inv, dots))
    inv_ref[...] = both
    inv, dots = both[:, 0:1], both[:, 1:2]
    normed = attention_ref[...] * inv
    grad = grad_ref[...].astype(jnp.float32)
    grad_attn = (inv * (grad * gain_ref[...] - normed * dots)).astype(jnp.bfloat16)
    grad_attn_ref[...] = grad_attn
    gain = jnp.sum(grad * normed, axis=0, keepdims=True)
    gain = jnp.transpose(jnp.broadcast_to(gain, (8, gain.shape[1])))
    queued = query_ref[...].astype(jnp.float32) * over_features(cols_ref[...], 0, BLOCK)
    write_pieces(queued.astype(jnp.bfloat16), grad_attn, rows_ref, gain[:, 0:1], pieces_ref)


def inside_back_kernel(
    rows_ref, cols_ref, query_ref, key_ref, value_ref, probs_ref, grad_attn_ref, states_ref,
    attention_ref, inv_ref, gain_ref,
    grad_query_ref, part_key_ref, part_value_ref, attended_ref,
):
    grad_attn, value = grad_attn_ref[...], value_ref[...]
    weights = []
    for h, mask in decay_masks(rows_ref, cols_ref):
        low, high = WINDOWS[h]
        grads = dot(only_head(grad_attn, h), value[:, low * TILE : high * TILE], 1, 1)
        weights.append((grads * mask).astype(jnp.bfloat16))
    high, low = read_states(states_ref)
    outer = dot(grad_attn, high, 1, 1) + dot(grad_attn, low, 1, 1)
    grad_query = times_heads(weights, key_ref[...], 1) + outer * over_features(cols_ref[...], 0, BLOCK)
    grad_query_ref[...] = grad_query.astype(jnp.bfloat16)
    part_key_ref[...] = times_heads(weights, query_ref[...], 0)
    part_value_ref[...] = times_heads([probs_ref[h] for h in range(HEADS)], grad_attn, 0)
    attended = attention_ref[...] * inv_ref[:, 0:1] * gain_ref[...]
    attended_ref[...] = attended.astype(jnp.bfloat16)


def last_kernel(
    scale, states_ref, cols_ref, key_ref, value_ref, part_key_ref, part_value_ref,
    grad_key_ref, grad_value_ref, grad_gain_ref,
):
    high, low = read_states(states_ref)
    tail = over_features(cols_ref[...], 4, BLOCK)
    key, value = key_ref[...], value_ref[...]
    outer = dot(value, high, 1, 1) + dot(value, low, 1, 1)
    grad_key_ref[...] = (part_key_ref[...] + outer * tail).astype(jnp.bfloat16)
    outer = dot(key, high) + dot(key, low)
    grad_value_ref[...] = (part_value_ref[...] + outer * tail).astype(jnp.bfloat16)
    count = states_ref.shape[0]
    gain = jnp.concatenate([states_ref[k] for k in range(count)], axis=0)
    grad_gain_ref[...] = (jnp.transpose(gain)[GAIN : GAIN + 1] * scale).reshape(gain.shape[0])


def scan_states(pieces, backward):
    group, sub, lanes = pieces.shape
    pieces = lax.all_to_all(pieces, "near", 0, 0, tiled=True)
    group_count = lax.axis_size("wide")
    (total,) = on_chip(
        functools.partial(total_kernel, backward),
        [pltpu.VMEM((group_count, sub, lanes), jnp.float32)],
        [pieces],
        "group_total",
    )
    groups = lax.all_to_all(total, "wide", 0, 0, tiled=True)
    (states,) = on_chip(
        functools.partial(prefix_kernel, backward),
        [pltpu.VMEM((group, sub, lanes), jnp.float32)],
        [pieces, groups],
        "group_prefix",
    )
    return lax.all_to_all(states, "near", 0, 0, tiled=True)


def local(queries, key_rows, values, log_decay, segment_ids, norm_gain, grad_out):
    tokens, features = queries.shape
    group = lax.axis_size("near")
    dp_count = lax.axis_size("wide") * group
    fsdp = lax.axis_size("fsdp")
    full = (tokens, features)
    mxu = 2 * tokens * tokens * HEAD * HEADS
    pieces, rows, cols = on_chip(
        summary_kernel,
        [
            pltpu.VMEM((group, SUB, TILE), jnp.float32),
            pltpu.VMEM((8, tokens), jnp.float32),
            pltpu.VMEM((tokens, 16), jnp.float32),
        ],
        [segment_ids, log_decay, key_rows, values],
        "summary",
        flops=mxu,
        held_in=pltpu.HBM,
    )
    probs, inner = on_chip(
        inside_kernel,
        [pltpu.VMEM((HEADS, tokens, tokens), jnp.bfloat16), pltpu.VMEM(full, jnp.float32)],
        [rows, cols, queries, key_rows, values],
        "inside",
        flops=4 * mxu,
        exps=HEADS * tokens * tokens,
    )
    state_in = scan_states(pieces, False)
    gain_row = norm_gain.reshape(1, features)
    attention, sums = on_chip(
        attention_kernel,
        [pltpu.VMEM(full, jnp.float32), pltpu.VMEM((fsdp, 2, tokens), jnp.float32)],
        [state_in, inner, cols, queries, grad_out, gain_row],
        "attention",
        flops=2 * mxu,
    )
    sums = lax.all_to_all(sums, "fsdp", 0, 0, tiled=True)
    grad_attn, inv, back_pieces = on_chip(
        functools.partial(gradient_kernel, features * fsdp),
        [
            pltpu.VMEM(full, jnp.bfloat16),
            pltpu.VMEM((tokens, 8), jnp.float32),
            pltpu.VMEM((group, SUB, TILE), jnp.float32),
        ],
        [sums, attention, grad_out, gain_row, rows, cols, queries],
        "gradient",
        flops=mxu,
    )
    grad_queries, part_key, part_value, attended = on_chip(
        inside_back_kernel,
        [
            jax.ShapeDtypeStruct(full, jnp.bfloat16),
            pltpu.VMEM(full, jnp.float32),
            pltpu.VMEM(full, jnp.float32),
            jax.ShapeDtypeStruct(full, jnp.bfloat16),
        ],
        [rows, cols, queries, key_rows, values, probs, grad_attn, state_in, attention, inv, gain_row],
        "inside_back",
        flops=8 * mxu,
        exps=HEADS * tokens * tokens,
    )
    back_in = scan_states(back_pieces, True)
    grad_keys, grad_values, grad_gain = on_chip(
        functools.partial(last_kernel, float(tokens * dp_count) ** (-0.5)),
        [
            jax.ShapeDtypeStruct(full, jnp.bfloat16),
            jax.ShapeDtypeStruct(full, jnp.bfloat16),
            jax.ShapeDtypeStruct((features,), jnp.float32),
        ],
        [back_in, cols, key_rows, values, part_key, part_value],
        "last",
        flops=4 * mxu,
    )
    return (attended, grad_queries, grad_keys, grad_values, grad_gain)


def columns(ref, count):
    picked = [[ref[k, :, lane : lane + 1] for k in range(count)] for lane in (PASS, NEAR, FAR)]
    return picked


def total_kernel(backward, pieces_ref, out_ref):
    count, rows, lanes = pieces_ref.shape
    order = list(range(count))[::-1] if backward else list(range(count))
    passes, near, far = columns(pieces_ref, count)
    if backward:
        near, far = far, near
    lane = lax.broadcasted_iota(jnp.int32, (rows, lanes), 1)
    running = pieces_ref[order[0]]
    gain = running
    through = passes[order[0]]
    for before, k in zip(order[:-1], order[1:]):
        piece = pieces_ref[k]
        carried = passes[k] * (far[before] == near[k]).astype(jnp.float32)
        running = piece + carried * running
        through = through * carried
        gain = gain + piece
    first, last = order[0], order[-1]
    out = jnp.where(lane < PASS, running, gain)
    out = jnp.where(lane == PASS, through, out)
    out = jnp.where(lane == NEAR, near[first], out)
    out = jnp.where(lane == FAR, far[last], out)
    for g in range(out_ref.shape[0]):
        out_ref[g] = out


def prefix_kernel(backward, pieces_ref, groups_ref, out_ref):
    count, rows, lanes = pieces_ref.shape
    group_count = groups_ref.shape[0]
    mine = lax.axis_index("wide")
    lane = lax.broadcasted_iota(jnp.int32, (rows, lanes), 1)
    group_order = list(range(group_count))[::-1] if backward else list(range(group_count))
    running = jnp.zeros((rows, lanes), jnp.float32)
    gain = jnp.zeros((rows, lanes), jnp.float32)
    last_far = jnp.full((rows, 1), -1.0, jnp.float32)
    entering = running
    entering_far = last_far
    for g in group_order:
        here = mine == g
        entering = jnp.where(here, running, entering)
        entering_far = jnp.where(here, last_far, entering_far)
        piece = groups_ref[g]
        joined = (last_far == piece[:, NEAR : NEAR + 1]).astype(jnp.float32)
        running = piece + (piece[:, PASS : PASS + 1] * joined) * running
        gain = gain + piece
        last_far = piece[:, FAR : FAR + 1]
    order = list(range(count))[::-1] if backward else list(range(count))
    passes, near, far = columns(pieces_ref, count)
    if backward:
        near, far = far, near
    state = entering
    before_far = entering_far
    for k in order:
        joined = (before_far == near[k]).astype(jnp.float32)
        state = state * joined
        out_ref[k] = jnp.where(lane < PASS, state, gain)
        state = pieces_ref[k] + passes[k] * state
        before_far = far[k]


def solution(mesh):
    dp_count, fsdp_count = mesh.devices.shape
    near_count = 16
    fine = Mesh(
        mesh.devices.reshape(dp_count // near_count, near_count, fsdp_count),
        ("wide", "near", "fsdp"),
    )
    dp = ("wide", "near")
    return jax.shard_map(
        local,
        mesh=fine,
        in_specs=(
            P(dp, "fsdp"),
            P(dp, "fsdp"),
            P(dp, "fsdp"),
            P("fsdp", dp),
            P(dp),
            P("fsdp"),
            P(dp, "fsdp"),
        ),
        out_specs=(P(dp, "fsdp"), P(dp, "fsdp"), P(dp, "fsdp"), P(dp, "fsdp"), P("fsdp")),
        check_vma=False,
    )
```

```python
import functools

import jax
import jax.numpy as jnp
from jax import lax
from jax.experimental import pallas as pl
from jax.experimental.pallas import tpu as pltpu
from jax.sharding import Mesh
from jax.sharding import PartitionSpec as P

BLOCK = 256
EPSILON = 1e-06
PRECISE = lax.Precision.HIGHEST
PASS, NEAR, FAR, GAIN = 96, 97, 98, 99


HEADS, HEAD, TILE = 4, 96, 128
SUB = 24
STARTS = tuple(HEAD * h % TILE for h in range(HEADS))
WINDOWS = tuple((HEAD * h // TILE, (HEAD * h + HEAD - 1) // TILE + 1) for h in range(HEADS))


def on_chip(kernel, outs, operands, name, flops=0, exps=0, held_in=pltpu.VMEM):
    placed, specs, moved = [], [], 0
    for x in operands:
        placed.append(pltpu.with_memory_space_constraint(x, held_in))
        inside = pltpu.SMEM if x.dtype == jnp.int32 else pltpu.VMEM
        specs.append(pl.BlockSpec(memory_space=inside))
        moved += x.size * x.dtype.itemsize
    for out in outs:
        moved += out.size * out.dtype.itemsize if hasattr(out, "size") else 0
    return pl.pallas_call(
        kernel,
        out_shape=outs,
        in_specs=specs,
        out_specs=[pl.BlockSpec(memory_space=pltpu.VMEM) for _ in outs],
        cost_estimate=pl.CostEstimate(
            flops=flops, bytes_accessed=moved, transcendentals=exps
        ),
        compiler_params=pltpu.CompilerParams(vmem_limit_bytes=40 * 1024 * 1024),
        name=name,
    )(*placed)


def dot(a, b, over_a=1, over_b=0):
    return lax.dot_general(
        a, b, (((over_a,), (over_b,)), ((), ())), preferred_element_type=jnp.float32
    )


def row_of(ref):
    return ref[...].reshape(1, ref.shape[0])


def pick_heads(parts, tile, rows):
    lane = lax.broadcasted_iota(jnp.int32, (rows, TILE), 1) + tile * TILE
    inside = [h for h in range(HEADS) if WINDOWS[h][0] <= tile < WINDOWS[h][1]]
    out = parts[inside[-1]]
    for h in inside[:-1][::-1]:
        out = jnp.where(lane < HEAD * (h + 1), parts[h], out)
    return out


def over_features(cols, first, rows):
    spread = [jnp.broadcast_to(cols[:, first + h : first + h + 1], (rows, TILE)) for h in range(HEADS)]
    return jnp.concatenate([pick_heads(spread, c, rows) for c in range(3)], axis=1)


def only_head(x, h):
    low, high = WINDOWS[h]
    x = x[:, low * TILE : high * TILE]
    lane = lax.broadcasted_iota(jnp.int32, x.shape, 1) + low * TILE
    inside = jnp.logical_and(lane >= HEAD * h, lane < HEAD * (h + 1))
    return jnp.where(inside, x, jnp.zeros_like(x))


def write_pieces(left, right, rows_ref, gain, out_ref):
    full = dot(left, right, 0, 0)
    lane = lax.broadcasted_iota(jnp.int32, (HEAD, TILE), 1)
    last = BLOCK - 1
    same, near, far = (rows_ref[r : r + 1, last:] for r in (4, 5, 6))
    for h in range(HEADS):
        low, high = WINDOWS[h]
        tiles = [full[HEAD * h : HEAD * (h + 1), TILE * c : TILE * (c + 1)] for c in range(low, high)]
        state = tiles[0] if len(tiles) == 1 else jnp.where(lane >= STARTS[h], tiles[0], tiles[1])
        if STARTS[h]:
            state = pltpu.roll(state, TILE - STARTS[h], 1)
        through = jnp.exp(rows_ref[h : h + 1, last:]) * same
        state = jnp.where(lane < HEAD, state, through)
        state = jnp.where(lane == NEAR, near, state)
        state = jnp.where(lane == FAR, far, state)
        state = jnp.where(lane == GAIN, 0.0 if gain is None else gain[HEAD * h : HEAD * (h + 1)], state)
        for i in range(HEAD // SUB):
            out_ref[h * (HEAD // SUB) + i] = state[i * SUB : (i + 1) * SUB]


def read_states(pieces_ref):
    lane = lax.broadcasted_iota(jnp.int32, (HEAD, TILE), 1)
    zero = jnp.zeros((HEAD, TILE), jnp.float32)
    parts = HEAD // SUB
    bands = []
    for h in range(HEADS):
        state = jnp.concatenate([pieces_ref[h * parts + i] for i in range(parts)], axis=0)
        state = jnp.where(lane < HEAD, state, 0.0)
        if STARTS[h]:
            state = pltpu.roll(state, STARTS[h], 1)
        low, high = WINDOWS[h]
        tiles = [zero] * 3
        if high - low == 1:
            tiles[low] = state
        else:
            tiles[low] = jnp.where(lane >= STARTS[h], state, 0.0)
            tiles[low + 1] = jnp.where(lane >= STARTS[h], 0.0, state)
        bands.append(jnp.concatenate(tiles, axis=1))
    whole = jnp.concatenate(bands, axis=0)
    high = whole.astype(jnp.bfloat16)
    return high, (whole - high.astype(jnp.float32)).astype(jnp.bfloat16)


def summary_kernel(segment_ref, decay_ref, key_ref, value_ref, pieces_ref, rows_ref, cols_ref):
    near, far = segment_ref[0], segment_ref[BLOCK - 1]
    same = (near == far).astype(jnp.float32)
    earlier = lax.broadcasted_iota(jnp.int32, (BLOCK, BLOCK), 0) <= lax.broadcasted_iota(
        jnp.int32, (BLOCK, BLOCK), 1
    )
    decay = decay_ref[...]
    decay = jnp.concatenate([decay, decay], axis=0)
    cumulative = jnp.dot(
        decay, earlier.astype(jnp.float32), precision=PRECISE, preferred_element_type=jnp.float32
    )
    row = lax.broadcasted_iota(jnp.int32, (8, BLOCK), 0)
    first_half = lax.broadcasted_iota(jnp.int32, (8, BLOCK), 1) < BLOCK // 2
    last = cumulative[:, BLOCK - 1 :]
    in_near = jnp.where(first_half, 1.0, same)
    in_far = jnp.where(first_half, same, 1.0)
    decays = jnp.where(
        row < HEADS, jnp.exp(cumulative) * in_near, jnp.exp(last - cumulative) * in_far
    )
    tags = jnp.where(row == 4, same, jnp.where(row == 5, near.astype(jnp.float32), far.astype(jnp.float32)))
    rows_ref[...] = jnp.where(row < HEADS, cumulative, tags)
    cols = jnp.transpose(jnp.concatenate([decays, cumulative], axis=0))
    cols_ref[...] = cols
    keyed = key_ref[...].astype(jnp.float32) * over_features(cols, 4, BLOCK)
    write_pieces(keyed.astype(jnp.bfloat16), value_ref[...], rows_ref, None, pieces_ref)


def decay_masks(rows_ref, cols_ref):
    t = lax.broadcasted_iota(jnp.int32, (BLOCK, BLOCK), 0)
    s = lax.broadcasted_iota(jnp.int32, (BLOCK, BLOCK), 1)
    half = BLOCK // 2
    together = jnp.logical_or((t < half) == (s < half), rows_ref[4:5, :] > 0.5)
    allowed = jnp.logical_and(t >= s, together)
    for h in range(HEADS):
        gap = cols_ref[:, 8 + h : 9 + h] - rows_ref[h : h + 1, :]
        yield h, jnp.exp(jnp.where(allowed, gap, -1e30))


def times_heads(weights, x, over):
    tiles = []
    for c in range(3):
        column = x[:, c * TILE : (c + 1) * TILE]
        parts = [
            dot(weights[h], column, over, 0) if WINDOWS[h][0] <= c < WINDOWS[h][1] else None
            for h in range(HEADS)
        ]
        tiles.append(pick_heads(parts, c, BLOCK))
    return jnp.concatenate(tiles, axis=1)


def inside_kernel(rows_ref, cols_ref, query_ref, key_ref, value_ref, probs_ref, inner_ref, ready_ref):
    query, key = query_ref[...], key_ref[...]
    weights = []
    for h, mask in decay_masks(rows_ref, cols_ref):
        low, high = WINDOWS[h]
        scores = dot(only_head(query, h), key[:, low * TILE : high * TILE], 1, 1)
        weights.append((scores * mask).astype(jnp.bfloat16))
        probs_ref[h] = weights[h]
    inner_ref[...] = times_heads(weights, value_ref[...], 1)
    ready_ref[...] = jnp.zeros(ready_ref.shape, jnp.float32)


def attention_kernel(
    states_ref, inner_ref, cols_ref, query_ref, grad_ref, gain_ref, attention_ref, sums_ref
):
    high, low = read_states(states_ref)
    query = query_ref[...]
    outer = dot(query, high) + dot(query, low)
    attention = inner_ref[...] + outer * over_features(cols_ref[...], 0, BLOCK)
    attention_ref[...] = attention
    squares = attention * attention
    products = grad_ref[...].astype(jnp.float32) * row_of(gain_ref) * attention
    sums = []
    for x in (squares, products):
        x = x[:, :TILE] + x[:, TILE : 2 * TILE] + x[:, 2 * TILE :]
        sums.append(jnp.sum(jnp.transpose(x), axis=0, keepdims=True))
    sums = jnp.concatenate(sums, axis=0)
    for k in range(sums_ref.shape[0]):
        sums_ref[k] = sums


def gradient_kernel(
    width, sums_ref, attention_ref, grad_ref, gain_ref, rows_ref, cols_ref, query_ref,
    grad_attn_ref, inv_ref, pieces_ref,
):
    sums = sums_ref[0]
    for k in range(1, sums_ref.shape[0]):
        sums = sums + sums_ref[k]
    inv = lax.rsqrt(sums[0:1] / width + EPSILON)
    dots = sums[1:2] * inv / width
    row = lax.broadcasted_iota(jnp.int32, (8, BLOCK), 0)
    both = jnp.transpose(jnp.where(row == 0, inv, dots))
    inv_ref[...] = both
    inv, dots = both[:, 0:1], both[:, 1:2]
    normed = attention_ref[...] * inv
    grad = grad_ref[...].astype(jnp.float32)
    grad_attn = (inv * (grad * row_of(gain_ref) - normed * dots)).astype(jnp.bfloat16)
    grad_attn_ref[...] = grad_attn
    gain = jnp.sum(grad * normed, axis=0, keepdims=True)
    gain = jnp.transpose(jnp.broadcast_to(gain, (8, gain.shape[1])))
    queued = query_ref[...].astype(jnp.float32) * over_features(cols_ref[...], 0, BLOCK)
    write_pieces(queued.astype(jnp.bfloat16), grad_attn, rows_ref, gain[:, 0:1], pieces_ref)


def inside_back_kernel(
    rows_ref, cols_ref, query_ref, key_ref, value_ref, probs_ref, grad_attn_ref, states_ref,
    attention_ref, inv_ref, gain_ref,
    grad_query_ref, part_key_ref, part_value_ref, attended_ref, ready_ref,
):
    grad_attn, value = grad_attn_ref[...], value_ref[...]
    weights = []
    for h, mask in decay_masks(rows_ref, cols_ref):
        low, high = WINDOWS[h]
        grads = dot(only_head(grad_attn, h), value[:, low * TILE : high * TILE], 1, 1)
        weights.append((grads * mask).astype(jnp.bfloat16))
    high, low = read_states(states_ref)
    outer = dot(grad_attn, high, 1, 1) + dot(grad_attn, low, 1, 1)
    grad_query = times_heads(weights, key_ref[...], 1) + outer * over_features(cols_ref[...], 0, BLOCK)
    grad_query_ref[...] = grad_query.astype(jnp.bfloat16)
    part_key_ref[...] = times_heads(weights, query_ref[...], 0)
    part_value_ref[...] = times_heads([probs_ref[h] for h in range(HEADS)], grad_attn, 0)
    attended = attention_ref[...] * inv_ref[:, 0:1] * row_of(gain_ref)
    attended_ref[...] = attended.astype(jnp.bfloat16)
    ready_ref[...] = jnp.zeros(ready_ref.shape, jnp.float32)


def last_kernel(
    scale, states_ref, cols_ref, key_ref, value_ref, part_key_ref, part_value_ref,
    grad_key_ref, grad_value_ref, grad_gain_ref,
):
    high, low = read_states(states_ref)
    tail = over_features(cols_ref[...], 4, BLOCK)
    key, value = key_ref[...], value_ref[...]
    outer = dot(value, high, 1, 1) + dot(value, low, 1, 1)
    grad_key_ref[...] = (part_key_ref[...] + outer * tail).astype(jnp.bfloat16)
    outer = dot(key, high) + dot(key, low)
    grad_value_ref[...] = (part_value_ref[...] + outer * tail).astype(jnp.bfloat16)
    count = states_ref.shape[0]
    gain = jnp.concatenate([states_ref[k] for k in range(count)], axis=0)
    grad_gain_ref[...] = (jnp.transpose(gain)[GAIN : GAIN + 1] * scale).reshape(gain.shape[0])


def reach_owners(pieces, backward):
    group, sub, lanes = pieces.shape
    pieces = lax.all_to_all(pieces, "near", 0, 0, tiled=True)
    (total,) = on_chip(
        functools.partial(total_kernel, backward),
        [pltpu.VMEM((lax.axis_size("wide"), sub, lanes), jnp.float32)],
        [pieces],
        "group_total",
    )
    groups = lax.all_to_all(total, "wide", 0, 0, tiled=True)
    inside = on_chip(
        functools.partial(local_prefix_kernel, backward),
        [pltpu.VMEM(pieces.shape, jnp.float32), pltpu.VMEM(pieces.shape, jnp.float32)],
        [pieces],
        "local_prefix",
        flops=8 * pieces.size,
    )
    return (*inside, groups)


def leave_owners(local_states, factors, groups, ready, backward):
    (states,) = on_chip(
        functools.partial(prefix_kernel, backward),
        [pltpu.VMEM(local_states.shape, jnp.float32)],
        [local_states, factors, groups, ready],
        "group_prefix",
    )
    return lax.all_to_all(states, "near", 0, 0, tiled=True)


def local(queries, key_rows, values, log_decay, segment_ids, norm_gain, grad_out):
    tokens, features = queries.shape
    group = lax.axis_size("near")
    dp_count = lax.axis_size("wide") * group
    fsdp = lax.axis_size("fsdp")
    full = (tokens, features)
    mxu = 2 * tokens * tokens * HEAD * HEADS
    pieces, rows, cols = on_chip(
        summary_kernel,
        [
            pltpu.VMEM((group, SUB, TILE), jnp.float32),
            pltpu.VMEM((8, tokens), jnp.float32),
            pltpu.VMEM((tokens, 16), jnp.float32),
        ],
        [segment_ids, log_decay, key_rows, values],
        "summary",
        flops=mxu,
        held_in=pltpu.HBM,
    )
    scan = reach_owners(pieces, False)
    ready_shape = pltpu.VMEM((8, TILE), jnp.float32)
    probs, inner, ready = on_chip(
        inside_kernel,
        [
            pltpu.VMEM((HEADS, tokens, tokens), jnp.bfloat16),
            pltpu.VMEM(full, jnp.float32),
            ready_shape,
        ],
        [rows, cols, queries, key_rows, values],
        "inside",
        flops=4 * mxu,
        exps=HEADS * tokens * tokens,
    )
    state_in = leave_owners(*scan, ready, False)
    attention, sums = on_chip(
        attention_kernel,
        [pltpu.VMEM(full, jnp.float32), pltpu.VMEM((fsdp, 2, tokens), jnp.float32)],
        [state_in, inner, cols, queries, grad_out, norm_gain],
        "attention",
        flops=2 * mxu,
    )
    sums = lax.all_to_all(sums, "fsdp", 0, 0, tiled=True)
    grad_attn, inv, back_pieces = on_chip(
        functools.partial(gradient_kernel, features * fsdp),
        [
            pltpu.VMEM(full, jnp.bfloat16),
            pltpu.VMEM((tokens, 8), jnp.float32),
            pltpu.VMEM((group, SUB, TILE), jnp.float32),
        ],
        [sums, attention, grad_out, norm_gain, rows, cols, queries],
        "gradient",
        flops=mxu,
    )
    back_scan = reach_owners(back_pieces, True)
    grad_queries, part_key, part_value, attended, back_ready = on_chip(
        inside_back_kernel,
        [
            jax.ShapeDtypeStruct(full, jnp.bfloat16),
            pltpu.VMEM(full, jnp.float32),
            pltpu.VMEM(full, jnp.float32),
            jax.ShapeDtypeStruct(full, jnp.bfloat16),
            ready_shape,
        ],
        [rows, cols, queries, key_rows, values, probs, grad_attn, state_in, attention, inv, norm_gain],
        "inside_back",
        flops=8 * mxu,
        exps=HEADS * tokens * tokens,
    )
    back_in = leave_owners(*back_scan, back_ready, True)
    grad_keys, grad_values, grad_gain = on_chip(
        functools.partial(last_kernel, float(tokens * dp_count) ** (-0.5)),
        [
            jax.ShapeDtypeStruct(full, jnp.bfloat16),
            jax.ShapeDtypeStruct(full, jnp.bfloat16),
            jax.ShapeDtypeStruct((features,), jnp.float32),
        ],
        [back_in, cols, key_rows, values, part_key, part_value],
        "last",
        flops=4 * mxu,
    )
    return (attended, grad_queries, grad_keys, grad_values, grad_gain)


def columns(ref, count):
    picked = [[ref[k, :, lane : lane + 1] for k in range(count)] for lane in (PASS, NEAR, FAR)]
    return picked


def total_kernel(backward, pieces_ref, out_ref):
    count, rows, lanes = pieces_ref.shape
    order = list(range(count))[::-1] if backward else list(range(count))
    passes, near, far = columns(pieces_ref, count)
    if backward:
        near, far = far, near
    lane = lax.broadcasted_iota(jnp.int32, (rows, lanes), 1)
    running = pieces_ref[order[0]]
    gain = running
    through = passes[order[0]]
    for before, k in zip(order[:-1], order[1:]):
        piece = pieces_ref[k]
        carried = passes[k] * (far[before] == near[k]).astype(jnp.float32)
        running = piece + carried * running
        through = through * carried
        gain = gain + piece
    first, last = order[0], order[-1]
    out = jnp.where(lane < PASS, running, gain)
    out = jnp.where(lane == PASS, through, out)
    out = jnp.where(lane == NEAR, near[first], out)
    out = jnp.where(lane == FAR, far[last], out)
    for g in range(out_ref.shape[0]):
        out_ref[g] = out


def local_prefix_kernel(backward, pieces_ref, local_ref, factor_ref):
    count, rows, lanes = pieces_ref.shape
    order = list(range(count))[::-1] if backward else list(range(count))
    passes, near, far = columns(pieces_ref, count)
    if backward:
        near, far = far, near
    state = jnp.zeros((rows, lanes), jnp.float32)
    factor = jnp.ones((rows, lanes), jnp.float32)
    local_ref[order[0]] = state
    factor_ref[order[0]] = factor
    for before, k in zip(order[:-1], order[1:]):
        joined = (far[before] == near[k]).astype(jnp.float32)
        carried = jnp.broadcast_to(passes[before] * joined, (rows, lanes))
        state = pieces_ref[before] * joined + carried * state
        factor = carried * factor
        local_ref[k] = state
        factor_ref[k] = factor


def prefix_kernel(backward, local_ref, factor_ref, groups_ref, ready_ref, out_ref):
    del ready_ref
    count, rows, lanes = local_ref.shape
    group_count = groups_ref.shape[0]
    mine = lax.axis_index("wide")
    lane = lax.broadcasted_iota(jnp.int32, (rows, lanes), 1)
    running = jnp.zeros((rows, lanes), jnp.float32)
    gain = jnp.zeros((rows, lanes), jnp.float32)
    entering = running
    order = list(range(group_count))[::-1] if backward else list(range(group_count))
    passes, near, far = columns(groups_ref, group_count)
    for at, g in enumerate(order):
        if at:
            running = running * (far[order[at - 1]] == near[g]).astype(jnp.float32)
        entering = jnp.where(mine == g, running, entering)
        piece = groups_ref[g]
        running = piece + passes[g] * running
        gain = gain + piece
    states = [jnp.where(lane < PASS, local_ref[k] + factor_ref[k] * entering, gain) for k in range(count)]
    for k in range(count):
        out_ref[k] = states[k]


def solution(mesh):
    dp_count, fsdp_count = mesh.devices.shape
    near_count = 16
    fine = Mesh(
        mesh.devices.reshape(dp_count // near_count, near_count, fsdp_count),
        ("wide", "near", "fsdp"),
    )
    dp = ("wide", "near")
    return jax.shard_map(
        local,
        mesh=fine,
        in_specs=(
            P(dp, "fsdp"),
            P(dp, "fsdp"),
            P(dp, "fsdp"),
            P("fsdp", dp),
            P(dp),
            P("fsdp"),
            P(dp, "fsdp"),
        ),
        out_specs=(P(dp, "fsdp"), P(dp, "fsdp"), P(dp, "fsdp"), P(dp, "fsdp"), P("fsdp")),
        check_vma=False,
    )
```

```python
import functools

import jax
import jax.numpy as jnp
from jax import lax
from jax.experimental import pallas as pl
from jax.experimental.pallas import tpu as pltpu
from jax.sharding import Mesh
from jax.sharding import PartitionSpec as P

BLOCK = 256
EPSILON = 1e-06
PRECISE = lax.Precision.HIGHEST
PASS, NEAR, FAR, GAIN = 96, 97, 98, 99


HEADS, HEAD, TILE = 4, 96, 128
SUB = 24
NEAR_ORDER = (5, 1, 2, 3, 4, 0, 6, 7, 8, 9, 10, 11, 12, 13, 14, 15)
WIDE_ORDER = (4, 5, 6, 7, 0, 1, 2, 3)
STARTS = tuple(HEAD * h % TILE for h in range(HEADS))
WINDOWS = tuple((HEAD * h // TILE, (HEAD * h + HEAD - 1) // TILE + 1) for h in range(HEADS))


def exchange(x, axis, order):
    return lax.all_to_all(x, axis, 0, 0, axis_index_groups=[list(order)], tiled=True)


def places(order, backward):
    found = [order.index(k) for k in range(len(order))]
    return found[::-1] if backward else found


def on_chip(kernel, outs, operands, name, flops=0, exps=0, held_in=pltpu.VMEM):
    placed, specs, moved = [], [], 0
    for x in operands:
        placed.append(pltpu.with_memory_space_constraint(x, held_in))
        inside = pltpu.SMEM if x.dtype == jnp.int32 else pltpu.VMEM
        specs.append(pl.BlockSpec(memory_space=inside))
        moved += x.size * x.dtype.itemsize
    for out in outs:
        moved += out.size * out.dtype.itemsize if hasattr(out, "size") else 0
    return pl.pallas_call(
        kernel,
        out_shape=outs,
        in_specs=specs,
        out_specs=[pl.BlockSpec(memory_space=pltpu.VMEM) for _ in outs],
        cost_estimate=pl.CostEstimate(
            flops=flops, bytes_accessed=moved, transcendentals=exps
        ),
        compiler_params=pltpu.CompilerParams(vmem_limit_bytes=40 * 1024 * 1024),
        name=name,
    )(*placed)


def dot(a, b, over_a=1, over_b=0):
    return lax.dot_general(
        a, b, (((over_a,), (over_b,)), ((), ())), preferred_element_type=jnp.float32
    )


def row_of(ref):
    return ref[...].reshape(1, ref.shape[0])


def pick_heads(parts, tile, rows):
    lane = lax.broadcasted_iota(jnp.int32, (rows, TILE), 1) + tile * TILE
    inside = [h for h in range(HEADS) if WINDOWS[h][0] <= tile < WINDOWS[h][1]]
    out = parts[inside[-1]]
    for h in inside[:-1][::-1]:
        out = jnp.where(lane < HEAD * (h + 1), parts[h], out)
    return out


def over_features(cols, first, rows):
    spread = [jnp.broadcast_to(cols[:, first + h : first + h + 1], (rows, TILE)) for h in range(HEADS)]
    return jnp.concatenate([pick_heads(spread, c, rows) for c in range(3)], axis=1)


def only_head(x, h):
    low, high = WINDOWS[h]
    x = x[:, low * TILE : high * TILE]
    lane = lax.broadcasted_iota(jnp.int32, x.shape, 1) + low * TILE
    inside = jnp.logical_and(lane >= HEAD * h, lane < HEAD * (h + 1))
    return jnp.where(inside, x, jnp.zeros_like(x))


def write_pieces(left, right, rows_ref, gain, out_ref):
    full = dot(left, right, 0, 0)
    lane = lax.broadcasted_iota(jnp.int32, (HEAD, TILE), 1)
    last = BLOCK - 1
    same, near, far = (rows_ref[r : r + 1, last:] for r in (4, 5, 6))
    for h in range(HEADS):
        low, high = WINDOWS[h]
        tiles = [full[HEAD * h : HEAD * (h + 1), TILE * c : TILE * (c + 1)] for c in range(low, high)]
        state = tiles[0] if len(tiles) == 1 else jnp.where(lane >= STARTS[h], tiles[0], tiles[1])
        if STARTS[h]:
            state = pltpu.roll(state, TILE - STARTS[h], 1)
        through = jnp.exp(rows_ref[h : h + 1, last:]) * same
        state = jnp.where(lane < HEAD, state, through)
        state = jnp.where(lane == NEAR, near, state)
        state = jnp.where(lane == FAR, far, state)
        state = jnp.where(lane == GAIN, 0.0 if gain is None else gain[HEAD * h : HEAD * (h + 1)], state)
        for i in range(HEAD // SUB):
            out_ref[h * (HEAD // SUB) + i] = state[i * SUB : (i + 1) * SUB]


def read_states(pieces_ref):
    lane = lax.broadcasted_iota(jnp.int32, (HEAD, TILE), 1)
    zero = jnp.zeros((HEAD, TILE), jnp.float32)
    parts = HEAD // SUB
    bands = []
    for h in range(HEADS):
        state = jnp.concatenate([pieces_ref[h * parts + i] for i in range(parts)], axis=0)
        state = jnp.where(lane < HEAD, state, 0.0)
        if STARTS[h]:
            state = pltpu.roll(state, STARTS[h], 1)
        low, high = WINDOWS[h]
        tiles = [zero] * 3
        if high - low == 1:
            tiles[low] = state
        else:
            tiles[low] = jnp.where(lane >= STARTS[h], state, 0.0)
            tiles[low + 1] = jnp.where(lane >= STARTS[h], 0.0, state)
        bands.append(jnp.concatenate(tiles, axis=1))
    whole = jnp.concatenate(bands, axis=0)
    high = whole.astype(jnp.bfloat16)
    return high, (whole - high.astype(jnp.float32)).astype(jnp.bfloat16)


def summary_kernel(segment_ref, decay_ref, key_ref, value_ref, pieces_ref, rows_ref, cols_ref):
    near, far = segment_ref[0], segment_ref[BLOCK - 1]
    same = (near == far).astype(jnp.float32)
    earlier = lax.broadcasted_iota(jnp.int32, (BLOCK, BLOCK), 0) <= lax.broadcasted_iota(
        jnp.int32, (BLOCK, BLOCK), 1
    )
    decay = decay_ref[...]
    decay = jnp.concatenate([decay, decay], axis=0)
    cumulative = jnp.dot(
        decay, earlier.astype(jnp.float32), precision=PRECISE, preferred_element_type=jnp.float32
    )
    row = lax.broadcasted_iota(jnp.int32, (8, BLOCK), 0)
    first_half = lax.broadcasted_iota(jnp.int32, (8, BLOCK), 1) < BLOCK // 2
    last = cumulative[:, BLOCK - 1 :]
    in_near = jnp.where(first_half, 1.0, same)
    in_far = jnp.where(first_half, same, 1.0)
    decays = jnp.where(
        row < HEADS, jnp.exp(cumulative) * in_near, jnp.exp(last - cumulative) * in_far
    )
    tags = jnp.where(row == 4, same, jnp.where(row == 5, near.astype(jnp.float32), far.astype(jnp.float32)))
    rows_ref[...] = jnp.where(row < HEADS, cumulative, tags)
    cols = jnp.transpose(jnp.concatenate([decays, cumulative], axis=0))
    cols_ref[...] = cols
    keyed = key_ref[...].astype(jnp.float32) * over_features(cols, 4, BLOCK)
    write_pieces(keyed.astype(jnp.bfloat16), value_ref[...], rows_ref, None, pieces_ref)


def decay_masks(rows_ref, cols_ref):
    t = lax.broadcasted_iota(jnp.int32, (BLOCK, BLOCK), 0)
    s = lax.broadcasted_iota(jnp.int32, (BLOCK, BLOCK), 1)
    half = BLOCK // 2
    together = jnp.logical_or((t < half) == (s < half), rows_ref[4:5, :] > 0.5)
    allowed = jnp.logical_and(t >= s, together)
    for h in range(HEADS):
        gap = cols_ref[:, 8 + h : 9 + h] - rows_ref[h : h + 1, :]
        yield h, jnp.exp(jnp.where(allowed, gap, -1e30))


def times_heads(weights, x, over):
    tiles = []
    for c in range(3):
        column = x[:, c * TILE : (c + 1) * TILE]
        parts = [
            dot(weights[h], column, over, 0) if WINDOWS[h][0] <= c < WINDOWS[h][1] else None
            for h in range(HEADS)
        ]
        tiles.append(pick_heads(parts, c, BLOCK))
    return jnp.concatenate(tiles, axis=1)


def inside_kernel(rows_ref, cols_ref, query_ref, key_ref, value_ref, probs_ref, inner_ref, ready_ref):
    query, key = query_ref[...], key_ref[...]
    weights = []
    for h, mask in decay_masks(rows_ref, cols_ref):
        low, high = WINDOWS[h]
        scores = dot(only_head(query, h), key[:, low * TILE : high * TILE], 1, 1)
        weights.append((scores * mask).astype(jnp.bfloat16))
        probs_ref[h] = weights[h]
    inner_ref[...] = times_heads(weights, value_ref[...], 1)
    ready_ref[...] = jnp.zeros(ready_ref.shape, jnp.float32)


def attention_kernel(
    states_ref, inner_ref, cols_ref, query_ref, grad_ref, gain_ref, attention_ref, sums_ref
):
    high, low = read_states(states_ref)
    query = query_ref[...]
    outer = dot(query, high) + dot(query, low)
    attention = inner_ref[...] + outer * over_features(cols_ref[...], 0, BLOCK)
    attention_ref[...] = attention
    squares = attention * attention
    products = grad_ref[...].astype(jnp.float32) * row_of(gain_ref) * attention
    sums = []
    for x in (squares, products):
        x = x[:, :TILE] + x[:, TILE : 2 * TILE] + x[:, 2 * TILE :]
        sums.append(jnp.sum(jnp.transpose(x), axis=0, keepdims=True))
    sums = jnp.concatenate(sums, axis=0)
    for k in range(sums_ref.shape[0]):
        sums_ref[k] = sums


def gradient_kernel(
    width, sums_ref, attention_ref, grad_ref, gain_ref, rows_ref, cols_ref, query_ref,
    grad_attn_ref, inv_ref, pieces_ref,
):
    sums = sums_ref[0]
    for k in range(1, sums_ref.shape[0]):
        sums = sums + sums_ref[k]
    inv = lax.rsqrt(sums[0:1] / width + EPSILON)
    dots = sums[1:2] * inv / width
    row = lax.broadcasted_iota(jnp.int32, (8, BLOCK), 0)
    both = jnp.transpose(jnp.where(row == 0, inv, dots))
    inv_ref[...] = both
    inv, dots = both[:, 0:1], both[:, 1:2]
    normed = attention_ref[...] * inv
    grad = grad_ref[...].astype(jnp.float32)
    grad_attn = (inv * (grad * row_of(gain_ref) - normed * dots)).astype(jnp.bfloat16)
    grad_attn_ref[...] = grad_attn
    gain = jnp.sum(grad * normed, axis=0, keepdims=True)
    gain = jnp.transpose(jnp.broadcast_to(gain, (8, gain.shape[1])))
    queued = query_ref[...].astype(jnp.float32) * over_features(cols_ref[...], 0, BLOCK)
    write_pieces(queued.astype(jnp.bfloat16), grad_attn, rows_ref, gain[:, 0:1], pieces_ref)


def inside_back_kernel(
    rows_ref, cols_ref, query_ref, key_ref, value_ref, probs_ref, grad_attn_ref, states_ref,
    attention_ref, inv_ref, gain_ref,
    grad_query_ref, part_key_ref, part_value_ref, attended_ref, ready_ref,
):
    grad_attn, value = grad_attn_ref[...], value_ref[...]
    weights = []
    for h, mask in decay_masks(rows_ref, cols_ref):
        low, high = WINDOWS[h]
        grads = dot(only_head(grad_attn, h), value[:, low * TILE : high * TILE], 1, 1)
        weights.append((grads * mask).astype(jnp.bfloat16))
    high, low = read_states(states_ref)
    outer = dot(grad_attn, high, 1, 1) + dot(grad_attn, low, 1, 1)
    grad_query = times_heads(weights, key_ref[...], 1) + outer * over_features(cols_ref[...], 0, BLOCK)
    grad_query_ref[...] = grad_query.astype(jnp.bfloat16)
    part_key_ref[...] = times_heads(weights, query_ref[...], 0)
    part_value_ref[...] = times_heads([probs_ref[h] for h in range(HEADS)], grad_attn, 0)
    attended = attention_ref[...] * inv_ref[:, 0:1] * row_of(gain_ref)
    attended_ref[...] = attended.astype(jnp.bfloat16)
    ready_ref[...] = jnp.zeros(ready_ref.shape, jnp.float32)


def last_kernel(
    scale, states_ref, cols_ref, key_ref, value_ref, part_key_ref, part_value_ref,
    grad_key_ref, grad_value_ref, grad_gain_ref,
):
    high, low = read_states(states_ref)
    tail = over_features(cols_ref[...], 4, BLOCK)
    key, value = key_ref[...], value_ref[...]
    outer = dot(value, high, 1, 1) + dot(value, low, 1, 1)
    grad_key_ref[...] = (part_key_ref[...] + outer * tail).astype(jnp.bfloat16)
    outer = dot(key, high) + dot(key, low)
    grad_value_ref[...] = (part_value_ref[...] + outer * tail).astype(jnp.bfloat16)
    count = states_ref.shape[0]
    gain = jnp.concatenate([states_ref[k] for k in range(count)], axis=0)
    grad_gain_ref[...] = (jnp.transpose(gain)[GAIN : GAIN + 1] * scale).reshape(gain.shape[0])


def reach_owners(pieces, backward):
    group, sub, lanes = pieces.shape
    pieces = exchange(pieces, "near", NEAR_ORDER)
    (total,) = on_chip(
        functools.partial(total_kernel, backward),
        [pltpu.VMEM((lax.axis_size("wide"), sub, lanes), jnp.float32)],
        [pieces],
        "group_total",
    )
    groups = exchange(total, "wide", WIDE_ORDER)
    inside = on_chip(
        functools.partial(local_prefix_kernel, backward),
        [pltpu.VMEM(pieces.shape, jnp.float32), pltpu.VMEM(pieces.shape, jnp.float32)],
        [pieces],
        "local_prefix",
        flops=8 * pieces.size,
    )
    return (*inside, groups)


def leave_owners(local_states, factors, groups, ready, backward):
    (states,) = on_chip(
        functools.partial(prefix_kernel, backward),
        [pltpu.VMEM(local_states.shape, jnp.float32)],
        [local_states, factors, groups, ready],
        "group_prefix",
    )
    return exchange(states, "near", NEAR_ORDER)


def local(queries, key_rows, values, log_decay, segment_ids, norm_gain, grad_out):
    tokens, features = queries.shape
    group = lax.axis_size("near")
    dp_count = lax.axis_size("wide") * group
    fsdp = lax.axis_size("fsdp")
    full = (tokens, features)
    mxu = 2 * tokens * tokens * HEAD * HEADS
    pieces, rows, cols = on_chip(
        summary_kernel,
        [
            pltpu.VMEM((group, SUB, TILE), jnp.float32),
            pltpu.VMEM((8, tokens), jnp.float32),
            pltpu.VMEM((tokens, 16), jnp.float32),
        ],
        [segment_ids, log_decay, key_rows, values],
        "summary",
        flops=mxu,
        held_in=pltpu.HBM,
    )
    scan = reach_owners(pieces, False)
    ready_shape = pltpu.VMEM((8, TILE), jnp.float32)
    probs, inner, ready = on_chip(
        inside_kernel,
        [
            pltpu.VMEM((HEADS, tokens, tokens), jnp.bfloat16),
            pltpu.VMEM(full, jnp.float32),
            ready_shape,
        ],
        [rows, cols, queries, key_rows, values],
        "inside",
        flops=4 * mxu,
        exps=HEADS * tokens * tokens,
    )
    state_in = leave_owners(*scan, ready, False)
    attention, sums = on_chip(
        attention_kernel,
        [pltpu.VMEM(full, jnp.float32), pltpu.VMEM((fsdp, 2, tokens), jnp.float32)],
        [state_in, inner, cols, queries, grad_out, norm_gain],
        "attention",
        flops=2 * mxu,
    )
    sums = lax.all_to_all(sums, "fsdp", 0, 0, tiled=True)
    grad_attn, inv, back_pieces = on_chip(
        functools.partial(gradient_kernel, features * fsdp),
        [
            pltpu.VMEM(full, jnp.bfloat16),
            pltpu.VMEM((tokens, 8), jnp.float32),
            pltpu.VMEM((group, SUB, TILE), jnp.float32),
        ],
        [sums, attention, grad_out, norm_gain, rows, cols, queries],
        "gradient",
        flops=mxu,
    )
    back_scan = reach_owners(back_pieces, True)
    grad_queries, part_key, part_value, attended, back_ready = on_chip(
        inside_back_kernel,
        [
            jax.ShapeDtypeStruct(full, jnp.bfloat16),
            pltpu.VMEM(full, jnp.float32),
            pltpu.VMEM(full, jnp.float32),
            jax.ShapeDtypeStruct(full, jnp.bfloat16),
            ready_shape,
        ],
        [rows, cols, queries, key_rows, values, probs, grad_attn, state_in, attention, inv, norm_gain],
        "inside_back",
        flops=8 * mxu,
        exps=HEADS * tokens * tokens,
    )
    back_in = leave_owners(*back_scan, back_ready, True)
    grad_keys, grad_values, grad_gain = on_chip(
        functools.partial(last_kernel, float(tokens * dp_count) ** (-0.5)),
        [
            jax.ShapeDtypeStruct(full, jnp.bfloat16),
            jax.ShapeDtypeStruct(full, jnp.bfloat16),
            jax.ShapeDtypeStruct((features,), jnp.float32),
        ],
        [back_in, cols, key_rows, values, part_key, part_value],
        "last",
        flops=4 * mxu,
    )
    return (attended, grad_queries, grad_keys, grad_values, grad_gain)


def columns(ref, count):
    picked = [[ref[k, :, lane : lane + 1] for k in range(count)] for lane in (PASS, NEAR, FAR)]
    return picked


def total_kernel(backward, pieces_ref, out_ref):
    count, rows, lanes = pieces_ref.shape
    order = places(NEAR_ORDER, backward)
    passes, near, far = columns(pieces_ref, count)
    if backward:
        near, far = far, near
    lane = lax.broadcasted_iota(jnp.int32, (rows, lanes), 1)
    running = pieces_ref[order[0]]
    gain = running
    through = passes[order[0]]
    for before, k in zip(order[:-1], order[1:]):
        piece = pieces_ref[k]
        carried = passes[k] * (far[before] == near[k]).astype(jnp.float32)
        running = piece + carried * running
        through = through * carried
        gain = gain + piece
    first, last = order[0], order[-1]
    out = jnp.where(lane < PASS, running, gain)
    out = jnp.where(lane == PASS, through, out)
    out = jnp.where(lane == NEAR, near[first], out)
    out = jnp.where(lane == FAR, far[last], out)
    for g in range(out_ref.shape[0]):
        out_ref[g] = out


def local_prefix_kernel(backward, pieces_ref, local_ref, factor_ref):
    count, rows, lanes = pieces_ref.shape
    order = places(NEAR_ORDER, backward)
    passes, near, far = columns(pieces_ref, count)
    if backward:
        near, far = far, near
    state = jnp.zeros((rows, lanes), jnp.float32)
    factor = jnp.ones((rows, lanes), jnp.float32)
    local_ref[order[0]] = state
    factor_ref[order[0]] = factor
    for before, k in zip(order[:-1], order[1:]):
        joined = (far[before] == near[k]).astype(jnp.float32)
        carried = jnp.broadcast_to(passes[before] * joined, (rows, lanes))
        state = pieces_ref[before] * joined + carried * state
        factor = carried * factor
        local_ref[k] = state
        factor_ref[k] = factor


def prefix_kernel(backward, local_ref, factor_ref, groups_ref, ready_ref, out_ref):
    del ready_ref
    count, rows, lanes = local_ref.shape
    group_count = groups_ref.shape[0]
    mine = lax.axis_index("wide")
    lane = lax.broadcasted_iota(jnp.int32, (rows, lanes), 1)
    running = jnp.zeros((rows, lanes), jnp.float32)
    gain = jnp.zeros((rows, lanes), jnp.float32)
    entering = running
    order = places(WIDE_ORDER, backward)
    passes, near, far = columns(groups_ref, group_count)
    for at, g in enumerate(order):
        if at:
            running = running * (far[order[at - 1]] == near[g]).astype(jnp.float32)
        entering = jnp.where(mine == WIDE_ORDER[g], running, entering)
        piece = groups_ref[g]
        running = piece + passes[g] * running
        gain = gain + piece
    states = [jnp.where(lane < PASS, local_ref[k] + factor_ref[k] * entering, gain) for k in range(count)]
    for k in range(count):
        out_ref[k] = states[k]


def solution(mesh):
    dp_count, fsdp_count = mesh.devices.shape
    near_count = 16
    fine = Mesh(
        mesh.devices.reshape(dp_count // near_count, near_count, fsdp_count),
        ("wide", "near", "fsdp"),
    )
    dp = ("wide", "near")
    return jax.shard_map(
        local,
        mesh=fine,
        in_specs=(
            P(dp, "fsdp"),
            P(dp, "fsdp"),
            P(dp, "fsdp"),
            P("fsdp", dp),
            P(dp),
            P("fsdp"),
            P(dp, "fsdp"),
        ),
        out_specs=(P(dp, "fsdp"), P(dp, "fsdp"), P(dp, "fsdp"), P(dp, "fsdp"), P("fsdp")),
        check_vma=False,
    )
```

```python
import functools

import jax
import jax.numpy as jnp
from jax import lax
from jax.experimental import pallas as pl
from jax.experimental.pallas import tpu as pltpu
from jax.sharding import Mesh
from jax.sharding import PartitionSpec as P

BLOCK = 256
EPSILON = 1e-06
PRECISE = lax.Precision.HIGHEST
PASS, NEAR, FAR, GAIN = 96, 97, 98, 99


HEADS, HEAD, TILE = 4, 96, 128
SUB = 24
NEAR_ORDER = (5, 1, 2, 3, 4, 0, 6, 7, 8, 9, 10, 11, 12, 13, 14, 15)
WIDE_ORDER = (5, 6, 7, 0, 1, 2, 3, 4)
REACH = 4
STARTS = tuple(HEAD * h % TILE for h in range(HEADS))
WINDOWS = tuple((HEAD * h // TILE, (HEAD * h + HEAD - 1) // TILE + 1) for h in range(HEADS))


def exchange(x, axis, order):
    return lax.all_to_all(x, axis, 0, 0, axis_index_groups=[list(order)], tiled=True)


def places(order, backward):
    found = [order.index(k) for k in range(len(order))]
    return found[::-1] if backward else found


def on_chip(kernel, outs, operands, name, flops=0, exps=0, held_in=pltpu.VMEM):
    placed, specs, moved = [], [], 0
    for x in operands:
        placed.append(pltpu.with_memory_space_constraint(x, held_in))
        inside = pltpu.SMEM if x.dtype == jnp.int32 else pltpu.VMEM
        specs.append(pl.BlockSpec(memory_space=inside))
        moved += x.size * x.dtype.itemsize
    for out in outs:
        moved += out.size * out.dtype.itemsize if hasattr(out, "size") else 0
    return pl.pallas_call(
        kernel,
        out_shape=outs,
        in_specs=specs,
        out_specs=[pl.BlockSpec(memory_space=pltpu.VMEM) for _ in outs],
        cost_estimate=pl.CostEstimate(
            flops=flops, bytes_accessed=moved, transcendentals=exps
        ),
        compiler_params=pltpu.CompilerParams(vmem_limit_bytes=40 * 1024 * 1024),
        name=name,
    )(*placed)


def dot(a, b, over_a=1, over_b=0):
    return lax.dot_general(
        a, b, (((over_a,), (over_b,)), ((), ())), preferred_element_type=jnp.float32
    )


def row_of(ref):
    return ref[...].reshape(1, ref.shape[0])


def pick_heads(parts, tile, rows):
    lane = lax.broadcasted_iota(jnp.int32, (rows, TILE), 1) + tile * TILE
    inside = [h for h in range(HEADS) if WINDOWS[h][0] <= tile < WINDOWS[h][1]]
    out = parts[inside[-1]]
    for h in inside[:-1][::-1]:
        out = jnp.where(lane < HEAD * (h + 1), parts[h], out)
    return out


def over_features(cols, first, rows):
    spread = [jnp.broadcast_to(cols[:, first + h : first + h + 1], (rows, TILE)) for h in range(HEADS)]
    return jnp.concatenate([pick_heads(spread, c, rows) for c in range(3)], axis=1)


def only_head(x, h):
    low, high = WINDOWS[h]
    x = x[:, low * TILE : high * TILE]
    lane = lax.broadcasted_iota(jnp.int32, x.shape, 1) + low * TILE
    inside = jnp.logical_and(lane >= HEAD * h, lane < HEAD * (h + 1))
    return jnp.where(inside, x, jnp.zeros_like(x))


def write_pieces(left, right, rows_ref, gain, out_ref):
    full = dot(left, right, 0, 0)
    lane = lax.broadcasted_iota(jnp.int32, (HEAD, TILE), 1)
    last = BLOCK - 1
    same, near, far = (rows_ref[r : r + 1, last:] for r in (4, 5, 6))
    for h in range(HEADS):
        low, high = WINDOWS[h]
        tiles = [full[HEAD * h : HEAD * (h + 1), TILE * c : TILE * (c + 1)] for c in range(low, high)]
        state = tiles[0] if len(tiles) == 1 else jnp.where(lane >= STARTS[h], tiles[0], tiles[1])
        if STARTS[h]:
            state = pltpu.roll(state, TILE - STARTS[h], 1)
        through = jnp.exp(rows_ref[h : h + 1, last:]) * same
        state = jnp.where(lane < HEAD, state, through)
        state = jnp.where(lane == NEAR, near, state)
        state = jnp.where(lane == FAR, far, state)
        state = jnp.where(lane == GAIN, 0.0 if gain is None else gain[HEAD * h : HEAD * (h + 1)], state)
        for i in range(HEAD // SUB):
            out_ref[h * (HEAD // SUB) + i] = state[i * SUB : (i + 1) * SUB]


def read_states(pieces_ref):
    lane = lax.broadcasted_iota(jnp.int32, (HEAD, TILE), 1)
    zero = jnp.zeros((HEAD, TILE), jnp.float32)
    parts = HEAD // SUB
    bands = []
    for h in range(HEADS):
        state = jnp.concatenate([pieces_ref[h * parts + i] for i in range(parts)], axis=0)
        state = jnp.where(lane < HEAD, state, 0.0)
        if STARTS[h]:
            state = pltpu.roll(state, STARTS[h], 1)
        low, high = WINDOWS[h]
        tiles = [zero] * 3
        if high - low == 1:
            tiles[low] = state
        else:
            tiles[low] = jnp.where(lane >= STARTS[h], state, 0.0)
            tiles[low + 1] = jnp.where(lane >= STARTS[h], 0.0, state)
        bands.append(jnp.concatenate(tiles, axis=1))
    whole = jnp.concatenate(bands, axis=0)
    high = whole.astype(jnp.bfloat16)
    return high, (whole - high.astype(jnp.float32)).astype(jnp.bfloat16)


def summary_kernel(segment_ref, decay_ref, key_ref, value_ref, pieces_ref, rows_ref, cols_ref):
    near, far = segment_ref[0], segment_ref[BLOCK - 1]
    same = (near == far).astype(jnp.float32)
    earlier = lax.broadcasted_iota(jnp.int32, (BLOCK, BLOCK), 0) <= lax.broadcasted_iota(
        jnp.int32, (BLOCK, BLOCK), 1
    )
    decay = decay_ref[...]
    decay = jnp.concatenate([decay, decay], axis=0)
    cumulative = jnp.dot(
        decay, earlier.astype(jnp.float32), precision=PRECISE, preferred_element_type=jnp.float32
    )
    row = lax.broadcasted_iota(jnp.int32, (8, BLOCK), 0)
    first_half = lax.broadcasted_iota(jnp.int32, (8, BLOCK), 1) < BLOCK // 2
    last = cumulative[:, BLOCK - 1 :]
    in_near = jnp.where(first_half, 1.0, same)
    in_far = jnp.where(first_half, same, 1.0)
    decays = jnp.where(
        row < HEADS, jnp.exp(cumulative) * in_near, jnp.exp(last - cumulative) * in_far
    )
    tags = jnp.where(row == 4, same, jnp.where(row == 5, near.astype(jnp.float32), far.astype(jnp.float32)))
    rows_ref[...] = jnp.where(row < HEADS, cumulative, tags)
    cols = jnp.transpose(jnp.concatenate([decays, cumulative], axis=0))
    cols_ref[...] = cols
    keyed = key_ref[...].astype(jnp.float32) * over_features(cols, 4, BLOCK)
    write_pieces(keyed.astype(jnp.bfloat16), value_ref[...], rows_ref, None, pieces_ref)


def decay_masks(rows_ref, cols_ref):
    t = lax.broadcasted_iota(jnp.int32, (BLOCK, BLOCK), 0)
    s = lax.broadcasted_iota(jnp.int32, (BLOCK, BLOCK), 1)
    half = BLOCK // 2
    together = jnp.logical_or((t < half) == (s < half), rows_ref[4:5, :] > 0.5)
    allowed = jnp.logical_and(t >= s, together)
    for h in range(HEADS):
        gap = cols_ref[:, 8 + h : 9 + h] - rows_ref[h : h + 1, :]
        yield h, jnp.exp(jnp.where(allowed, gap, -1e30))


def times_heads(weights, x, over):
    tiles = []
    for c in range(3):
        column = x[:, c * TILE : (c + 1) * TILE]
        parts = [
            dot(weights[h], column, over, 0) if WINDOWS[h][0] <= c < WINDOWS[h][1] else None
            for h in range(HEADS)
        ]
        tiles.append(pick_heads(parts, c, BLOCK))
    return jnp.concatenate(tiles, axis=1)


def inside_kernel(rows_ref, cols_ref, query_ref, key_ref, value_ref, probs_ref, inner_ref, ready_ref):
    query, key = query_ref[...], key_ref[...]
    weights = []
    for h, mask in decay_masks(rows_ref, cols_ref):
        low, high = WINDOWS[h]
        scores = dot(only_head(query, h), key[:, low * TILE : high * TILE], 1, 1)
        weights.append((scores * mask).astype(jnp.bfloat16))
        probs_ref[h] = weights[h]
    inner_ref[...] = times_heads(weights, value_ref[...], 1)
    ready_ref[...] = jnp.zeros(ready_ref.shape, jnp.float32)


def attention_kernel(
    states_ref, inner_ref, cols_ref, query_ref, grad_ref, gain_ref, attention_ref, sums_ref
):
    high, low = read_states(states_ref)
    query = query_ref[...]
    outer = dot(query, high) + dot(query, low)
    attention = inner_ref[...] + outer * over_features(cols_ref[...], 0, BLOCK)
    attention_ref[...] = attention
    squares = attention * attention
    products = grad_ref[...].astype(jnp.float32) * row_of(gain_ref) * attention
    sums = []
    for x in (squares, products):
        x = x[:, :TILE] + x[:, TILE : 2 * TILE] + x[:, 2 * TILE :]
        sums.append(jnp.sum(jnp.transpose(x), axis=0, keepdims=True))
    sums = jnp.concatenate(sums, axis=0)
    for k in range(sums_ref.shape[0]):
        sums_ref[k] = sums


def gradient_kernel(
    width, sums_ref, attention_ref, grad_ref, gain_ref, rows_ref, cols_ref, query_ref,
    grad_attn_ref, inv_ref, pieces_ref,
):
    sums = sums_ref[0]
    for k in range(1, sums_ref.shape[0]):
        sums = sums + sums_ref[k]
    inv = lax.rsqrt(sums[0:1] / width + EPSILON)
    dots = sums[1:2] * inv / width
    row = lax.broadcasted_iota(jnp.int32, (8, BLOCK), 0)
    both = jnp.transpose(jnp.where(row == 0, inv, dots))
    inv_ref[...] = both
    inv, dots = both[:, 0:1], both[:, 1:2]
    normed = attention_ref[...] * inv
    grad = grad_ref[...].astype(jnp.float32)
    grad_attn = (inv * (grad * row_of(gain_ref) - normed * dots)).astype(jnp.bfloat16)
    grad_attn_ref[...] = grad_attn
    gain = jnp.sum(grad * normed, axis=0, keepdims=True)
    gain = jnp.transpose(jnp.broadcast_to(gain, (8, gain.shape[1])))
    queued = query_ref[...].astype(jnp.float32) * over_features(cols_ref[...], 0, BLOCK)
    write_pieces(queued.astype(jnp.bfloat16), grad_attn, rows_ref, gain[:, 0:1], pieces_ref)


def inside_back_kernel(
    rows_ref, cols_ref, query_ref, key_ref, value_ref, probs_ref, grad_attn_ref, states_ref,
    attention_ref, inv_ref, gain_ref,
    grad_query_ref, part_key_ref, part_value_ref, attended_ref, ready_ref,
):
    grad_attn, value = grad_attn_ref[...], value_ref[...]
    weights = []
    for h, mask in decay_masks(rows_ref, cols_ref):
        low, high = WINDOWS[h]
        grads = dot(only_head(grad_attn, h), value[:, low * TILE : high * TILE], 1, 1)
        weights.append((grads * mask).astype(jnp.bfloat16))
    high, low = read_states(states_ref)
    outer = dot(grad_attn, high, 1, 1) + dot(grad_attn, low, 1, 1)
    grad_query = times_heads(weights, key_ref[...], 1) + outer * over_features(cols_ref[...], 0, BLOCK)
    grad_query_ref[...] = grad_query.astype(jnp.bfloat16)
    part_key_ref[...] = times_heads(weights, query_ref[...], 0)
    part_value_ref[...] = times_heads([probs_ref[h] for h in range(HEADS)], grad_attn, 0)
    attended = attention_ref[...] * inv_ref[:, 0:1] * row_of(gain_ref)
    attended_ref[...] = attended.astype(jnp.bfloat16)
    ready_ref[...] = jnp.zeros(ready_ref.shape, jnp.float32)


def last_kernel(
    scale, states_ref, cols_ref, key_ref, value_ref, part_key_ref, part_value_ref,
    grad_key_ref, grad_value_ref, grad_gain_ref,
):
    high, low = read_states(states_ref)
    tail = over_features(cols_ref[...], 4, BLOCK)
    key, value = key_ref[...], value_ref[...]
    outer = dot(value, high, 1, 1) + dot(value, low, 1, 1)
    grad_key_ref[...] = (part_key_ref[...] + outer * tail).astype(jnp.bfloat16)
    outer = dot(key, high) + dot(key, low)
    grad_value_ref[...] = (part_value_ref[...] + outer * tail).astype(jnp.bfloat16)
    count = states_ref.shape[0]
    gain = jnp.concatenate([states_ref[k] for k in range(count)], axis=0)
    grad_gain_ref[...] = (jnp.transpose(gain)[GAIN : GAIN + 1] * scale).reshape(gain.shape[0])


def reach_owners(pieces, backward):
    group, sub, lanes = pieces.shape
    wide = lax.axis_size("wide")
    pieces = exchange(pieces, "near", NEAR_ORDER)
    (total,) = on_chip(
        functools.partial(total_kernel, backward),
        [pltpu.VMEM((wide, sub, lanes) if backward else (sub, lanes), jnp.float32)],
        [pieces],
        "group_total",
    )
    if backward:
        groups = [exchange(total, "wide", WIDE_ORDER)]
    else:
        groups = [total]
        for away in range(1, REACH + 1):
            pairs = [(g, g + away) for g in range(wide - away)]
            groups.append(lax.ppermute(total, "wide", pairs))
    inside = on_chip(
        functools.partial(local_prefix_kernel, backward),
        [pltpu.VMEM(pieces.shape, jnp.float32), pltpu.VMEM(pieces.shape, jnp.float32)],
        [pieces],
        "local_prefix",
        flops=8 * pieces.size,
    )
    return (*inside, groups)


def leave_owners(local_states, factors, groups, ready, backward):
    (states,) = on_chip(
        back_prefix_kernel if backward else prefix_kernel,
        [pltpu.VMEM(local_states.shape, jnp.float32)],
        [local_states, factors, ready, *groups],
        "group_prefix",
    )
    return exchange(states, "near", NEAR_ORDER)


def local(queries, key_rows, values, log_decay, segment_ids, norm_gain, grad_out):
    tokens, features = queries.shape
    group = lax.axis_size("near")
    dp_count = lax.axis_size("wide") * group
    fsdp = lax.axis_size("fsdp")
    full = (tokens, features)
    mxu = 2 * tokens * tokens * HEAD * HEADS
    pieces, rows, cols = on_chip(
        summary_kernel,
        [
            pltpu.VMEM((group, SUB, TILE), jnp.float32),
            pltpu.VMEM((8, tokens), jnp.float32),
            pltpu.VMEM((tokens, 16), jnp.float32),
        ],
        [segment_ids, log_decay, key_rows, values],
        "summary",
        flops=mxu,
        held_in=pltpu.HBM,
    )
    scan = reach_owners(pieces, False)
    ready_shape = pltpu.VMEM((8, TILE), jnp.float32)
    probs, inner, ready = on_chip(
        inside_kernel,
        [
            pltpu.VMEM((HEADS, tokens, tokens), jnp.bfloat16),
            pltpu.VMEM(full, jnp.float32),
            ready_shape,
        ],
        [rows, cols, queries, key_rows, values],
        "inside",
        flops=4 * mxu,
        exps=HEADS * tokens * tokens,
    )
    state_in = leave_owners(*scan, ready, False)
    attention, sums = on_chip(
        attention_kernel,
        [pltpu.VMEM(full, jnp.float32), pltpu.VMEM((fsdp, 2, tokens), jnp.float32)],
        [state_in, inner, cols, queries, grad_out, norm_gain],
        "attention",
        flops=2 * mxu,
    )
    sums = lax.all_to_all(sums, "fsdp", 0, 0, tiled=True)
    grad_attn, inv, back_pieces = on_chip(
        functools.partial(gradient_kernel, features * fsdp),
        [
            pltpu.VMEM(full, jnp.bfloat16),
            pltpu.VMEM((tokens, 8), jnp.float32),
            pltpu.VMEM((group, SUB, TILE), jnp.float32),
        ],
        [sums, attention, grad_out, norm_gain, rows, cols, queries],
        "gradient",
        flops=mxu,
    )
    back_scan = reach_owners(back_pieces, True)
    grad_queries, part_key, part_value, attended, back_ready = on_chip(
        inside_back_kernel,
        [
            jax.ShapeDtypeStruct(full, jnp.bfloat16),
            pltpu.VMEM(full, jnp.float32),
            pltpu.VMEM(full, jnp.float32),
            jax.ShapeDtypeStruct(full, jnp.bfloat16),
            ready_shape,
        ],
        [rows, cols, queries, key_rows, values, probs, grad_attn, state_in, attention, inv, norm_gain],
        "inside_back",
        flops=8 * mxu,
        exps=HEADS * tokens * tokens,
    )
    back_in = leave_owners(*back_scan, back_ready, True)
    grad_keys, grad_values, grad_gain = on_chip(
        functools.partial(last_kernel, float(tokens * dp_count) ** (-0.5)),
        [
            jax.ShapeDtypeStruct(full, jnp.bfloat16),
            jax.ShapeDtypeStruct(full, jnp.bfloat16),
            jax.ShapeDtypeStruct((features,), jnp.float32),
        ],
        [back_in, cols, key_rows, values, part_key, part_value],
        "last",
        flops=4 * mxu,
    )
    return (attended, grad_queries, grad_keys, grad_values, grad_gain)


def columns(ref, count):
    picked = [[ref[k, :, lane : lane + 1] for k in range(count)] for lane in (PASS, NEAR, FAR)]
    return picked


def total_kernel(backward, pieces_ref, out_ref):
    count, rows, lanes = pieces_ref.shape
    order = places(NEAR_ORDER, backward)
    passes, near, far = columns(pieces_ref, count)
    if backward:
        near, far = far, near
    lane = lax.broadcasted_iota(jnp.int32, (rows, lanes), 1)
    running = pieces_ref[order[0]]
    gain = running
    through = passes[order[0]]
    for before, k in zip(order[:-1], order[1:]):
        piece = pieces_ref[k]
        carried = passes[k] * (far[before] == near[k]).astype(jnp.float32)
        running = piece + carried * running
        through = through * carried
        gain = gain + piece
    first, last = order[0], order[-1]
    out = jnp.where(lane < PASS, running, gain)
    out = jnp.where(lane == PASS, through, out)
    out = jnp.where(lane == NEAR, near[first], out)
    out = jnp.where(lane == FAR, far[last], out)
    if not backward:
        out_ref[...] = out
        return
    for g in range(out_ref.shape[0]):
        out_ref[g] = out


def local_prefix_kernel(backward, pieces_ref, local_ref, factor_ref):
    count, rows, lanes = pieces_ref.shape
    order = places(NEAR_ORDER, backward)
    passes, near, far = columns(pieces_ref, count)
    if backward:
        near, far = far, near
    state = jnp.zeros((rows, lanes), jnp.float32)
    factor = jnp.ones((rows, lanes), jnp.float32)
    local_ref[order[0]] = state
    factor_ref[order[0]] = factor
    for before, k in zip(order[:-1], order[1:]):
        joined = (far[before] == near[k]).astype(jnp.float32)
        carried = jnp.broadcast_to(passes[before] * joined, (rows, lanes))
        state = pieces_ref[before] * joined + carried * state
        factor = carried * factor
        local_ref[k] = state
        factor_ref[k] = factor


def prefix_kernel(local_ref, factor_ref, ready_ref, own_ref, *refs):
    del ready_ref
    *group_refs, out_ref = refs
    count, rows, lanes = local_ref.shape
    mine = lax.axis_index("wide")
    running = jnp.zeros((rows, lanes), jnp.float32)
    before = jnp.full((rows, 1), -1.0, jnp.float32)
    for away in range(REACH, 0, -1):
        piece = group_refs[away - 1][...]
        joined = (before == piece[:, NEAR : NEAR + 1]).astype(jnp.float32)
        running = piece + (piece[:, PASS : PASS + 1] * joined) * running
        running = jnp.where(mine >= away, running, 0.0)
        before = piece[:, FAR : FAR + 1]
    entering = running * (before == own_ref[:, NEAR : NEAR + 1]).astype(jnp.float32)
    states = [local_ref[k] + factor_ref[k] * entering for k in range(count)]
    for k in range(count):
        out_ref[k] = states[k]


def back_prefix_kernel(local_ref, factor_ref, ready_ref, groups_ref, out_ref):
    del ready_ref
    count, rows, lanes = local_ref.shape
    group_count = groups_ref.shape[0]
    mine = lax.axis_index("wide")
    lane = lax.broadcasted_iota(jnp.int32, (rows, lanes), 1)
    running = jnp.zeros((rows, lanes), jnp.float32)
    gain = jnp.zeros((rows, lanes), jnp.float32)
    entering = running
    order = places(WIDE_ORDER, True)
    passes, near, far = columns(groups_ref, group_count)
    for at, g in enumerate(order):
        if at:
            running = running * (far[order[at - 1]] == near[g]).astype(jnp.float32)
        entering = jnp.where(mine == WIDE_ORDER[g], running, entering)
        piece = groups_ref[g]
        running = piece + passes[g] * running
        gain = gain + piece
    states = [jnp.where(lane < PASS, local_ref[k] + factor_ref[k] * entering, gain) for k in range(count)]
    for k in range(count):
        out_ref[k] = states[k]


def solution(mesh):
    dp_count, fsdp_count = mesh.devices.shape
    near_count = 16
    fine = Mesh(
        mesh.devices.reshape(dp_count // near_count, near_count, fsdp_count),
        ("wide", "near", "fsdp"),
    )
    dp = ("wide", "near")
    return jax.shard_map(
        local,
        mesh=fine,
        in_specs=(
            P(dp, "fsdp"),
            P(dp, "fsdp"),
            P(dp, "fsdp"),
            P("fsdp", dp),
            P(dp),
            P("fsdp"),
            P(dp, "fsdp"),
        ),
        out_specs=(P(dp, "fsdp"), P(dp, "fsdp"), P(dp, "fsdp"), P(dp, "fsdp"), P("fsdp")),
        check_vma=False,
    )
```

```python
import functools

import jax
import jax.numpy as jnp
from jax import lax
from jax.experimental import pallas as pl
from jax.experimental.pallas import tpu as pltpu
from jax.sharding import Mesh
from jax.sharding import PartitionSpec as P

BLOCK = 256
EPSILON = 1e-06
PRECISE = lax.Precision.HIGHEST
PASS, NEAR, FAR, GAIN = 96, 97, 98, 99


HEADS, HEAD, TILE = 4, 96, 128
SUB = 24
NEAR_ORDER = (5, 1, 2, 3, 4, 0, 6, 7, 8, 9, 10, 11, 12, 13, 14, 15)
FORWARD_WIDE_ORDER = (5, 6, 7, 0, 1, 2, 3, 4)
BACKWARD_WIDE_ORDER = (4, 5, 6, 7, 0, 1, 2, 3)
STARTS = tuple(HEAD * h % TILE for h in range(HEADS))
WINDOWS = tuple((HEAD * h // TILE, (HEAD * h + HEAD - 1) // TILE + 1) for h in range(HEADS))


def exchange(x, axis, order):
    return lax.all_to_all(x, axis, 0, 0, axis_index_groups=[list(order)], tiled=True)


def wide_order(backward):
    return BACKWARD_WIDE_ORDER if backward else FORWARD_WIDE_ORDER


def places(order, backward):
    found = [order.index(k) for k in range(len(order))]
    return found[::-1] if backward else found


def on_chip(kernel, outs, operands, name, flops=0, exps=0, held_in=pltpu.VMEM):
    placed, specs, moved = [], [], 0
    for x in operands:
        placed.append(pltpu.with_memory_space_constraint(x, held_in))
        inside = pltpu.SMEM if x.dtype == jnp.int32 else pltpu.VMEM
        specs.append(pl.BlockSpec(memory_space=inside))
        moved += x.size * x.dtype.itemsize
    for out in outs:
        moved += out.size * out.dtype.itemsize if hasattr(out, "size") else 0
    return pl.pallas_call(
        kernel,
        out_shape=outs,
        in_specs=specs,
        out_specs=[pl.BlockSpec(memory_space=pltpu.VMEM) for _ in outs],
        cost_estimate=pl.CostEstimate(
            flops=flops, bytes_accessed=moved, transcendentals=exps
        ),
        compiler_params=pltpu.CompilerParams(vmem_limit_bytes=40 * 1024 * 1024),
        name=name,
    )(*placed)


def dot(a, b, over_a=1, over_b=0):
    return lax.dot_general(
        a, b, (((over_a,), (over_b,)), ((), ())), preferred_element_type=jnp.float32
    )


def row_of(ref):
    return ref[...].reshape(1, ref.shape[0])


def pick_heads(parts, tile, rows):
    lane = lax.broadcasted_iota(jnp.int32, (rows, TILE), 1) + tile * TILE
    inside = [h for h in range(HEADS) if WINDOWS[h][0] <= tile < WINDOWS[h][1]]
    out = parts[inside[-1]]
    for h in inside[:-1][::-1]:
        out = jnp.where(lane < HEAD * (h + 1), parts[h], out)
    return out


def over_features(cols, first, rows):
    spread = [jnp.broadcast_to(cols[:, first + h : first + h + 1], (rows, TILE)) for h in range(HEADS)]
    return jnp.concatenate([pick_heads(spread, c, rows) for c in range(3)], axis=1)


def only_head(x, h):
    low, high = WINDOWS[h]
    x = x[:, low * TILE : high * TILE]
    lane = lax.broadcasted_iota(jnp.int32, x.shape, 1) + low * TILE
    inside = jnp.logical_and(lane >= HEAD * h, lane < HEAD * (h + 1))
    return jnp.where(inside, x, jnp.zeros_like(x))


def write_pieces(left, right, rows_ref, gain, out_ref):
    full = dot(left, right, 0, 0)
    lane = lax.broadcasted_iota(jnp.int32, (HEAD, TILE), 1)
    last = BLOCK - 1
    same, near, far = (rows_ref[r : r + 1, last:] for r in (4, 5, 6))
    for h in range(HEADS):
        low, high = WINDOWS[h]
        tiles = [full[HEAD * h : HEAD * (h + 1), TILE * c : TILE * (c + 1)] for c in range(low, high)]
        state = tiles[0] if len(tiles) == 1 else jnp.where(lane >= STARTS[h], tiles[0], tiles[1])
        if STARTS[h]:
            state = pltpu.roll(state, TILE - STARTS[h], 1)
        through = jnp.exp(rows_ref[h : h + 1, last:]) * same
        state = jnp.where(lane < HEAD, state, through)
        state = jnp.where(lane == NEAR, near, state)
        state = jnp.where(lane == FAR, far, state)
        state = jnp.where(lane == GAIN, 0.0 if gain is None else gain[HEAD * h : HEAD * (h + 1)], state)
        for i in range(HEAD // SUB):
            out_ref[h * (HEAD // SUB) + i] = state[i * SUB : (i + 1) * SUB]


def read_states(pieces_ref):
    lane = lax.broadcasted_iota(jnp.int32, (HEAD, TILE), 1)
    zero = jnp.zeros((HEAD, TILE), jnp.float32)
    parts = HEAD // SUB
    bands = []
    for h in range(HEADS):
        state = jnp.concatenate([pieces_ref[h * parts + i] for i in range(parts)], axis=0)
        state = jnp.where(lane < HEAD, state, 0.0)
        if STARTS[h]:
            state = pltpu.roll(state, STARTS[h], 1)
        low, high = WINDOWS[h]
        tiles = [zero] * 3
        if high - low == 1:
            tiles[low] = state
        else:
            tiles[low] = jnp.where(lane >= STARTS[h], state, 0.0)
            tiles[low + 1] = jnp.where(lane >= STARTS[h], 0.0, state)
        bands.append(jnp.concatenate(tiles, axis=1))
    whole = jnp.concatenate(bands, axis=0)
    high = whole.astype(jnp.bfloat16)
    return high, (whole - high.astype(jnp.float32)).astype(jnp.bfloat16)


def summary_kernel(segment_ref, decay_ref, key_ref, value_ref, pieces_ref, rows_ref, cols_ref):
    near, far = segment_ref[0], segment_ref[BLOCK - 1]
    same = (near == far).astype(jnp.float32)
    earlier = lax.broadcasted_iota(jnp.int32, (BLOCK, BLOCK), 0) <= lax.broadcasted_iota(
        jnp.int32, (BLOCK, BLOCK), 1
    )
    decay = decay_ref[...]
    decay = jnp.concatenate([decay, decay], axis=0)
    cumulative = jnp.dot(
        decay, earlier.astype(jnp.float32), precision=PRECISE, preferred_element_type=jnp.float32
    )
    row = lax.broadcasted_iota(jnp.int32, (8, BLOCK), 0)
    first_half = lax.broadcasted_iota(jnp.int32, (8, BLOCK), 1) < BLOCK // 2
    last = cumulative[:, BLOCK - 1 :]
    in_near = jnp.where(first_half, 1.0, same)
    in_far = jnp.where(first_half, same, 1.0)
    decays = jnp.where(
        row < HEADS, jnp.exp(cumulative) * in_near, jnp.exp(last - cumulative) * in_far
    )
    tags = jnp.where(row == 4, same, jnp.where(row == 5, near.astype(jnp.float32), far.astype(jnp.float32)))
    rows_ref[...] = jnp.where(row < HEADS, cumulative, tags)
    cols = jnp.transpose(jnp.concatenate([decays, cumulative], axis=0))
    cols_ref[...] = cols
    keyed = key_ref[...].astype(jnp.float32) * over_features(cols, 4, BLOCK)
    write_pieces(keyed.astype(jnp.bfloat16), value_ref[...], rows_ref, None, pieces_ref)


def decay_masks(rows_ref, cols_ref):
    t = lax.broadcasted_iota(jnp.int32, (BLOCK, BLOCK), 0)
    s = lax.broadcasted_iota(jnp.int32, (BLOCK, BLOCK), 1)
    half = BLOCK // 2
    together = jnp.logical_or((t < half) == (s < half), rows_ref[4:5, :] > 0.5)
    allowed = jnp.logical_and(t >= s, together)
    for h in range(HEADS):
        gap = cols_ref[:, 8 + h : 9 + h] - rows_ref[h : h + 1, :]
        yield h, jnp.exp(jnp.where(allowed, gap, -1e30))


def times_heads(weights, x, over):
    tiles = []
    for c in range(3):
        column = x[:, c * TILE : (c + 1) * TILE]
        parts = [
            dot(weights[h], column, over, 0) if WINDOWS[h][0] <= c < WINDOWS[h][1] else None
            for h in range(HEADS)
        ]
        tiles.append(pick_heads(parts, c, BLOCK))
    return jnp.concatenate(tiles, axis=1)


def inside_kernel(rows_ref, cols_ref, query_ref, key_ref, value_ref, probs_ref, inner_ref, ready_ref):
    query, key = query_ref[...], key_ref[...]
    weights = []
    for h, mask in decay_masks(rows_ref, cols_ref):
        low, high = WINDOWS[h]
        scores = dot(only_head(query, h), key[:, low * TILE : high * TILE], 1, 1)
        weights.append((scores * mask).astype(jnp.bfloat16))
        probs_ref[h] = weights[h]
    inner_ref[...] = times_heads(weights, value_ref[...], 1)
    ready_ref[...] = jnp.zeros(ready_ref.shape, jnp.float32)


def attention_kernel(
    states_ref, inner_ref, cols_ref, query_ref, grad_ref, gain_ref, attention_ref, sums_ref
):
    high, low = read_states(states_ref)
    query = query_ref[...]
    outer = dot(query, high) + dot(query, low)
    attention = inner_ref[...] + outer * over_features(cols_ref[...], 0, BLOCK)
    attention_ref[...] = attention
    squares = attention * attention
    products = grad_ref[...].astype(jnp.float32) * row_of(gain_ref) * attention
    sums = []
    for x in (squares, products):
        x = x[:, :TILE] + x[:, TILE : 2 * TILE] + x[:, 2 * TILE :]
        sums.append(jnp.sum(jnp.transpose(x), axis=0, keepdims=True))
    sums = jnp.concatenate(sums, axis=0)
    for k in range(sums_ref.shape[0]):
        sums_ref[k] = sums


def gradient_kernel(
    width, sums_ref, attention_ref, grad_ref, gain_ref, rows_ref, cols_ref, query_ref,
    grad_attn_ref, inv_ref, pieces_ref,
):
    sums = sums_ref[0]
    for k in range(1, sums_ref.shape[0]):
        sums = sums + sums_ref[k]
    inv = lax.rsqrt(sums[0:1] / width + EPSILON)
    dots = sums[1:2] * inv / width
    row = lax.broadcasted_iota(jnp.int32, (8, BLOCK), 0)
    both = jnp.transpose(jnp.where(row == 0, inv, dots))
    inv_ref[...] = both
    inv, dots = both[:, 0:1], both[:, 1:2]
    normed = attention_ref[...] * inv
    grad = grad_ref[...].astype(jnp.float32)
    grad_attn = (inv * (grad * row_of(gain_ref) - normed * dots)).astype(jnp.bfloat16)
    grad_attn_ref[...] = grad_attn
    gain = jnp.sum(grad * normed, axis=0, keepdims=True)
    gain = jnp.transpose(jnp.broadcast_to(gain, (8, gain.shape[1])))
    queued = query_ref[...].astype(jnp.float32) * over_features(cols_ref[...], 0, BLOCK)
    write_pieces(queued.astype(jnp.bfloat16), grad_attn, rows_ref, gain[:, 0:1], pieces_ref)


def inside_back_kernel(
    rows_ref, cols_ref, query_ref, key_ref, value_ref, probs_ref, grad_attn_ref, states_ref,
    attention_ref, inv_ref, gain_ref,
    grad_query_ref, part_key_ref, part_value_ref, attended_ref, ready_ref,
):
    grad_attn, value = grad_attn_ref[...], value_ref[...]
    weights = []
    for h, mask in decay_masks(rows_ref, cols_ref):
        low, high = WINDOWS[h]
        grads = dot(only_head(grad_attn, h), value[:, low * TILE : high * TILE], 1, 1)
        weights.append((grads * mask).astype(jnp.bfloat16))
    high, low = read_states(states_ref)
    outer = dot(grad_attn, high, 1, 1) + dot(grad_attn, low, 1, 1)
    grad_query = times_heads(weights, key_ref[...], 1) + outer * over_features(cols_ref[...], 0, BLOCK)
    grad_query_ref[...] = grad_query.astype(jnp.bfloat16)
    part_key_ref[...] = times_heads(weights, query_ref[...], 0)
    part_value_ref[...] = times_heads([probs_ref[h] for h in range(HEADS)], grad_attn, 0)
    attended = attention_ref[...] * inv_ref[:, 0:1] * row_of(gain_ref)
    attended_ref[...] = attended.astype(jnp.bfloat16)
    ready_ref[...] = jnp.zeros(ready_ref.shape, jnp.float32)


def last_kernel(
    scale, states_ref, cols_ref, key_ref, value_ref, part_key_ref, part_value_ref,
    grad_key_ref, grad_value_ref, grad_gain_ref,
):
    high, low = read_states(states_ref)
    tail = over_features(cols_ref[...], 4, BLOCK)
    key, value = key_ref[...], value_ref[...]
    outer = dot(value, high, 1, 1) + dot(value, low, 1, 1)
    grad_key_ref[...] = (part_key_ref[...] + outer * tail).astype(jnp.bfloat16)
    outer = dot(key, high) + dot(key, low)
    grad_value_ref[...] = (part_value_ref[...] + outer * tail).astype(jnp.bfloat16)
    count = states_ref.shape[0]
    gain = jnp.concatenate([states_ref[k] for k in range(count)], axis=0)
    grad_gain_ref[...] = (jnp.transpose(gain)[GAIN : GAIN + 1] * scale).reshape(gain.shape[0])


def reach_owners(pieces, backward):
    group, sub, lanes = pieces.shape
    pieces = exchange(pieces, "near", NEAR_ORDER)
    (total,) = on_chip(
        functools.partial(total_kernel, backward),
        [pltpu.VMEM((lax.axis_size("wide"), sub, lanes), jnp.float32)],
        [pieces],
        "group_total",
    )
    groups = exchange(total, "wide", wide_order(backward))
    inside = on_chip(
        functools.partial(local_prefix_kernel, backward),
        [pltpu.VMEM(pieces.shape, jnp.float32), pltpu.VMEM(pieces.shape, jnp.float32)],
        [pieces],
        "local_prefix",
        flops=8 * pieces.size,
    )
    return (*inside, groups)


def leave_owners(local_states, factors, groups, ready, backward):
    (states,) = on_chip(
        functools.partial(prefix_kernel, backward),
        [pltpu.VMEM(local_states.shape, jnp.float32)],
        [local_states, factors, groups, ready],
        "group_prefix",
    )
    return exchange(states, "near", NEAR_ORDER)


def local(queries, key_rows, values, log_decay, segment_ids, norm_gain, grad_out):
    tokens, features = queries.shape
    group = lax.axis_size("near")
    dp_count = lax.axis_size("wide") * group
    fsdp = lax.axis_size("fsdp")
    full = (tokens, features)
    mxu = 2 * tokens * tokens * HEAD * HEADS
    pieces, rows, cols = on_chip(
        summary_kernel,
        [
            pltpu.VMEM((group, SUB, TILE), jnp.float32),
            pltpu.VMEM((8, tokens), jnp.float32),
            pltpu.VMEM((tokens, 16), jnp.float32),
        ],
        [segment_ids, log_decay, key_rows, values],
        "summary",
        flops=mxu,
        held_in=pltpu.HBM,
    )
    scan = reach_owners(pieces, False)
    ready_shape = pltpu.VMEM((8, TILE), jnp.float32)
    probs, inner, ready = on_chip(
        inside_kernel,
        [
            pltpu.VMEM((HEADS, tokens, tokens), jnp.bfloat16),
            pltpu.VMEM(full, jnp.float32),
            ready_shape,
        ],
        [rows, cols, queries, key_rows, values],
        "inside",
        flops=4 * mxu,
        exps=HEADS * tokens * tokens,
    )
    state_in = leave_owners(*scan, ready, False)
    attention, sums = on_chip(
        attention_kernel,
        [pltpu.VMEM(full, jnp.float32), pltpu.VMEM((fsdp, 2, tokens), jnp.float32)],
        [state_in, inner, cols, queries, grad_out, norm_gain],
        "attention",
        flops=2 * mxu,
    )
    sums = lax.all_to_all(sums, "fsdp", 0, 0, tiled=True)
    grad_attn, inv, back_pieces = on_chip(
        functools.partial(gradient_kernel, features * fsdp),
        [
            pltpu.VMEM(full, jnp.bfloat16),
            pltpu.VMEM((tokens, 8), jnp.float32),
            pltpu.VMEM((group, SUB, TILE), jnp.float32),
        ],
        [sums, attention, grad_out, norm_gain, rows, cols, queries],
        "gradient",
        flops=mxu,
    )
    back_scan = reach_owners(back_pieces, True)
    grad_queries, part_key, part_value, attended, back_ready = on_chip(
        inside_back_kernel,
        [
            jax.ShapeDtypeStruct(full, jnp.bfloat16),
            pltpu.VMEM(full, jnp.float32),
            pltpu.VMEM(full, jnp.float32),
            jax.ShapeDtypeStruct(full, jnp.bfloat16),
            ready_shape,
        ],
        [rows, cols, queries, key_rows, values, probs, grad_attn, state_in, attention, inv, norm_gain],
        "inside_back",
        flops=8 * mxu,
        exps=HEADS * tokens * tokens,
    )
    back_in = leave_owners(*back_scan, back_ready, True)
    grad_keys, grad_values, grad_gain = on_chip(
        functools.partial(last_kernel, float(tokens * dp_count) ** (-0.5)),
        [
            jax.ShapeDtypeStruct(full, jnp.bfloat16),
            jax.ShapeDtypeStruct(full, jnp.bfloat16),
            jax.ShapeDtypeStruct((features,), jnp.float32),
        ],
        [back_in, cols, key_rows, values, part_key, part_value],
        "last",
        flops=4 * mxu,
    )
    return (attended, grad_queries, grad_keys, grad_values, grad_gain)


def columns(ref, count):
    picked = [[ref[k, :, lane : lane + 1] for k in range(count)] for lane in (PASS, NEAR, FAR)]
    return picked


def total_kernel(backward, pieces_ref, out_ref):
    count, rows, lanes = pieces_ref.shape
    order = places(NEAR_ORDER, backward)
    passes, near, far = columns(pieces_ref, count)
    if backward:
        near, far = far, near
    lane = lax.broadcasted_iota(jnp.int32, (rows, lanes), 1)
    running = pieces_ref[order[0]]
    gain = running
    through = passes[order[0]]
    for before, k in zip(order[:-1], order[1:]):
        piece = pieces_ref[k]
        carried = passes[k] * (far[before] == near[k]).astype(jnp.float32)
        running = piece + carried * running
        through = through * carried
        gain = gain + piece
    first, last = order[0], order[-1]
    out = jnp.where(lane < PASS, running, gain)
    out = jnp.where(lane == PASS, through, out)
    out = jnp.where(lane == NEAR, near[first], out)
    out = jnp.where(lane == FAR, far[last], out)
    for g in range(out_ref.shape[0]):
        out_ref[g] = out


def local_prefix_kernel(backward, pieces_ref, local_ref, factor_ref):
    count, rows, lanes = pieces_ref.shape
    order = places(NEAR_ORDER, backward)
    passes, near, far = columns(pieces_ref, count)
    if backward:
        near, far = far, near
    state = jnp.zeros((rows, lanes), jnp.float32)
    factor = jnp.ones((rows, lanes), jnp.float32)
    local_ref[order[0]] = state
    factor_ref[order[0]] = factor
    for before, k in zip(order[:-1], order[1:]):
        joined = (far[before] == near[k]).astype(jnp.float32)
        carried = jnp.broadcast_to(passes[before] * joined, (rows, lanes))
        state = pieces_ref[before] * joined + carried * state
        factor = carried * factor
        local_ref[k] = state
        factor_ref[k] = factor


def prefix_kernel(backward, local_ref, factor_ref, groups_ref, ready_ref, out_ref):
    del ready_ref
    count, rows, lanes = local_ref.shape
    group_count = groups_ref.shape[0]
    mine = lax.axis_index("wide")
    lane = lax.broadcasted_iota(jnp.int32, (rows, lanes), 1)
    running = jnp.zeros((rows, lanes), jnp.float32)
    gain = jnp.zeros((rows, lanes), jnp.float32)
    entering = running
    order = places(wide_order(backward), backward)
    passes, near, far = columns(groups_ref, group_count)
    for at, g in enumerate(order):
        if at:
            running = running * (far[order[at - 1]] == near[g]).astype(jnp.float32)
        entering = jnp.where(mine == wide_order(backward)[g], running, entering)
        piece = groups_ref[g]
        running = piece + passes[g] * running
        gain = gain + piece
    states = [jnp.where(lane < PASS, local_ref[k] + factor_ref[k] * entering, gain) for k in range(count)]
    for k in range(count):
        out_ref[k] = states[k]


def solution(mesh):
    dp_count, fsdp_count = mesh.devices.shape
    near_count = 16
    fine = Mesh(
        mesh.devices.reshape(dp_count // near_count, near_count, fsdp_count),
        ("wide", "near", "fsdp"),
    )
    dp = ("wide", "near")
    return jax.shard_map(
        local,
        mesh=fine,
        in_specs=(
            P(dp, "fsdp"),
            P(dp, "fsdp"),
            P(dp, "fsdp"),
            P("fsdp", dp),
            P(dp),
            P("fsdp"),
            P(dp, "fsdp"),
        ),
        out_specs=(P(dp, "fsdp"), P(dp, "fsdp"), P(dp, "fsdp"), P(dp, "fsdp"), P("fsdp")),
        check_vma=False,
    )
```

```python
import functools

import jax
import jax.numpy as jnp
from jax import lax
from jax.experimental import pallas as pl
from jax.experimental.pallas import tpu as pltpu
from jax.sharding import Mesh
from jax.sharding import PartitionSpec as P

BLOCK = 256
EPSILON = 1e-06
PRECISE = lax.Precision.HIGHEST
PASS, NEAR, FAR, GAIN = 96, 97, 98, 99


HEADS, HEAD, TILE = 4, 96, 128
SUB = 24
NEAR_ORDER = (5, 6, 7, 8, 9, 10, 11, 12, 13, 14, 15, 0, 1, 2, 3, 4)
FORWARD_WIDE_ORDER = (5, 6, 7, 0, 1, 2, 3, 4)
BACKWARD_WIDE_ORDER = (4, 5, 6, 7, 0, 1, 2, 3)
STARTS = tuple(HEAD * h % TILE for h in range(HEADS))
WINDOWS = tuple((HEAD * h // TILE, (HEAD * h + HEAD - 1) // TILE + 1) for h in range(HEADS))


def exchange(x, axis, order):
    return lax.all_to_all(x, axis, 0, 0, axis_index_groups=[list(order)], tiled=True)


def wide_order(backward):
    return BACKWARD_WIDE_ORDER if backward else FORWARD_WIDE_ORDER


def places(order, backward):
    found = [order.index(k) for k in range(len(order))]
    return found[::-1] if backward else found


def on_chip(kernel, outs, operands, name, flops=0, exps=0, held_in=pltpu.VMEM):
    placed, specs, moved = [], [], 0
    for x in operands:
        placed.append(pltpu.with_memory_space_constraint(x, held_in))
        inside = pltpu.SMEM if x.dtype == jnp.int32 else pltpu.VMEM
        specs.append(pl.BlockSpec(memory_space=inside))
        moved += x.size * x.dtype.itemsize
    for out in outs:
        moved += out.size * out.dtype.itemsize if hasattr(out, "size") else 0
    return pl.pallas_call(
        kernel,
        out_shape=outs,
        in_specs=specs,
        out_specs=[pl.BlockSpec(memory_space=pltpu.VMEM) for _ in outs],
        cost_estimate=pl.CostEstimate(
            flops=flops, bytes_accessed=moved, transcendentals=exps
        ),
        compiler_params=pltpu.CompilerParams(vmem_limit_bytes=40 * 1024 * 1024),
        name=name,
    )(*placed)


def dot(a, b, over_a=1, over_b=0):
    return lax.dot_general(
        a, b, (((over_a,), (over_b,)), ((), ())), preferred_element_type=jnp.float32
    )


def row_of(ref):
    return ref[...].reshape(1, ref.shape[0])


def pick_heads(parts, tile, rows):
    lane = lax.broadcasted_iota(jnp.int32, (rows, TILE), 1) + tile * TILE
    inside = [h for h in range(HEADS) if WINDOWS[h][0] <= tile < WINDOWS[h][1]]
    out = parts[inside[-1]]
    for h in inside[:-1][::-1]:
        out = jnp.where(lane < HEAD * (h + 1), parts[h], out)
    return out


def over_features(cols, first, rows):
    spread = [jnp.broadcast_to(cols[:, first + h : first + h + 1], (rows, TILE)) for h in range(HEADS)]
    return jnp.concatenate([pick_heads(spread, c, rows) for c in range(3)], axis=1)


def only_head(x, h):
    low, high = WINDOWS[h]
    x = x[:, low * TILE : high * TILE]
    lane = lax.broadcasted_iota(jnp.int32, x.shape, 1) + low * TILE
    inside = jnp.logical_and(lane >= HEAD * h, lane < HEAD * (h + 1))
    return jnp.where(inside, x, jnp.zeros_like(x))


def write_pieces(left, right, rows_ref, gain, out_ref):
    full = dot(left, right, 0, 0)
    lane = lax.broadcasted_iota(jnp.int32, (HEAD, TILE), 1)
    last = BLOCK - 1
    same, near, far = (rows_ref[r : r + 1, last:] for r in (4, 5, 6))
    for h in range(HEADS):
        low, high = WINDOWS[h]
        tiles = [full[HEAD * h : HEAD * (h + 1), TILE * c : TILE * (c + 1)] for c in range(low, high)]
        state = tiles[0] if len(tiles) == 1 else jnp.where(lane >= STARTS[h], tiles[0], tiles[1])
        if STARTS[h]:
            state = pltpu.roll(state, TILE - STARTS[h], 1)
        through = jnp.exp(rows_ref[h : h + 1, last:]) * same
        state = jnp.where(lane < HEAD, state, through)
        state = jnp.where(lane == NEAR, near, state)
        state = jnp.where(lane == FAR, far, state)
        state = jnp.where(lane == GAIN, 0.0 if gain is None else gain[HEAD * h : HEAD * (h + 1)], state)
        for i in range(HEAD // SUB):
            out_ref[h * (HEAD // SUB) + i] = state[i * SUB : (i + 1) * SUB]


def read_states(pieces_ref):
    lane = lax.broadcasted_iota(jnp.int32, (HEAD, TILE), 1)
    zero = jnp.zeros((HEAD, TILE), jnp.float32)
    parts = HEAD // SUB
    bands = []
    for h in range(HEADS):
        state = jnp.concatenate([pieces_ref[h * parts + i] for i in range(parts)], axis=0)
        state = jnp.where(lane < HEAD, state, 0.0)
        if STARTS[h]:
            state = pltpu.roll(state, STARTS[h], 1)
        low, high = WINDOWS[h]
        tiles = [zero] * 3
        if high - low == 1:
            tiles[low] = state
        else:
            tiles[low] = jnp.where(lane >= STARTS[h], state, 0.0)
            tiles[low + 1] = jnp.where(lane >= STARTS[h], 0.0, state)
        bands.append(jnp.concatenate(tiles, axis=1))
    whole = jnp.concatenate(bands, axis=0)
    high = whole.astype(jnp.bfloat16)
    return high, (whole - high.astype(jnp.float32)).astype(jnp.bfloat16)


def summary_kernel(segment_ref, decay_ref, key_ref, value_ref, pieces_ref, rows_ref, cols_ref):
    near, far = segment_ref[0], segment_ref[BLOCK - 1]
    same = (near == far).astype(jnp.float32)
    earlier = lax.broadcasted_iota(jnp.int32, (BLOCK, BLOCK), 0) <= lax.broadcasted_iota(
        jnp.int32, (BLOCK, BLOCK), 1
    )
    decay = decay_ref[...]
    decay = jnp.concatenate([decay, decay], axis=0)
    cumulative = jnp.dot(
        decay, earlier.astype(jnp.float32), precision=PRECISE, preferred_element_type=jnp.float32
    )
    row = lax.broadcasted_iota(jnp.int32, (8, BLOCK), 0)
    first_half = lax.broadcasted_iota(jnp.int32, (8, BLOCK), 1) < BLOCK // 2
    last = cumulative[:, BLOCK - 1 :]
    in_near = jnp.where(first_half, 1.0, same)
    in_far = jnp.where(first_half, same, 1.0)
    decays = jnp.where(
        row < HEADS, jnp.exp(cumulative) * in_near, jnp.exp(last - cumulative) * in_far
    )
    tags = jnp.where(row == 4, same, jnp.where(row == 5, near.astype(jnp.float32), far.astype(jnp.float32)))
    rows_ref[...] = jnp.where(row < HEADS, cumulative, tags)
    cols = jnp.transpose(jnp.concatenate([decays, cumulative], axis=0))
    cols_ref[...] = cols
    keyed = key_ref[...].astype(jnp.float32) * over_features(cols, 4, BLOCK)
    write_pieces(keyed.astype(jnp.bfloat16), value_ref[...], rows_ref, None, pieces_ref)


def decay_masks(rows_ref, cols_ref):
    t = lax.broadcasted_iota(jnp.int32, (BLOCK, BLOCK), 0)
    s = lax.broadcasted_iota(jnp.int32, (BLOCK, BLOCK), 1)
    half = BLOCK // 2
    together = jnp.logical_or((t < half) == (s < half), rows_ref[4:5, :] > 0.5)
    allowed = jnp.logical_and(t >= s, together)
    for h in range(HEADS):
        gap = cols_ref[:, 8 + h : 9 + h] - rows_ref[h : h + 1, :]
        yield h, jnp.exp(jnp.where(allowed, gap, -1e30))


def times_heads(weights, x, over):
    tiles = []
    for c in range(3):
        column = x[:, c * TILE : (c + 1) * TILE]
        parts = [
            dot(weights[h], column, over, 0) if WINDOWS[h][0] <= c < WINDOWS[h][1] else None
            for h in range(HEADS)
        ]
        tiles.append(pick_heads(parts, c, BLOCK))
    return jnp.concatenate(tiles, axis=1)


def inside_kernel(rows_ref, cols_ref, query_ref, key_ref, value_ref, probs_ref, inner_ref, ready_ref):
    query, key = query_ref[...], key_ref[...]
    weights = []
    for h, mask in decay_masks(rows_ref, cols_ref):
        low, high = WINDOWS[h]
        scores = dot(only_head(query, h), key[:, low * TILE : high * TILE], 1, 1)
        weights.append((scores * mask).astype(jnp.bfloat16))
        probs_ref[h] = weights[h]
    inner_ref[...] = times_heads(weights, value_ref[...], 1)
    ready_ref[...] = jnp.zeros(ready_ref.shape, jnp.float32)


def attention_kernel(
    states_ref, inner_ref, cols_ref, query_ref, grad_ref, gain_ref, attention_ref, sums_ref
):
    high, low = read_states(states_ref)
    query = query_ref[...]
    outer = dot(query, high) + dot(query, low)
    attention = inner_ref[...] + outer * over_features(cols_ref[...], 0, BLOCK)
    attention_ref[...] = attention
    squares = attention * attention
    products = grad_ref[...].astype(jnp.float32) * row_of(gain_ref) * attention
    sums = []
    for x in (squares, products):
        x = x[:, :TILE] + x[:, TILE : 2 * TILE] + x[:, 2 * TILE :]
        sums.append(jnp.sum(jnp.transpose(x), axis=0, keepdims=True))
    sums = jnp.concatenate(sums, axis=0)
    for k in range(sums_ref.shape[0]):
        sums_ref[k] = sums


def gradient_kernel(
    width, sums_ref, attention_ref, grad_ref, gain_ref, rows_ref, cols_ref, query_ref,
    grad_attn_ref, inv_ref, pieces_ref,
):
    sums = sums_ref[0]
    for k in range(1, sums_ref.shape[0]):
        sums = sums + sums_ref[k]
    inv = lax.rsqrt(sums[0:1] / width + EPSILON)
    dots = sums[1:2] * inv / width
    row = lax.broadcasted_iota(jnp.int32, (8, BLOCK), 0)
    both = jnp.transpose(jnp.where(row == 0, inv, dots))
    inv_ref[...] = both
    inv, dots = both[:, 0:1], both[:, 1:2]
    normed = attention_ref[...] * inv
    grad = grad_ref[...].astype(jnp.float32)
    grad_attn = (inv * (grad * row_of(gain_ref) - normed * dots)).astype(jnp.bfloat16)
    grad_attn_ref[...] = grad_attn
    gain = jnp.sum(grad * normed, axis=0, keepdims=True)
    gain = jnp.transpose(jnp.broadcast_to(gain, (8, gain.shape[1])))
    queued = query_ref[...].astype(jnp.float32) * over_features(cols_ref[...], 0, BLOCK)
    write_pieces(queued.astype(jnp.bfloat16), grad_attn, rows_ref, gain[:, 0:1], pieces_ref)


def inside_back_kernel(
    rows_ref, cols_ref, query_ref, key_ref, value_ref, probs_ref, grad_attn_ref, states_ref,
    attention_ref, inv_ref, gain_ref,
    grad_query_ref, part_key_ref, part_value_ref, attended_ref, ready_ref,
):
    grad_attn, value = grad_attn_ref[...], value_ref[...]
    weights = []
    for h, mask in decay_masks(rows_ref, cols_ref):
        low, high = WINDOWS[h]
        grads = dot(only_head(grad_attn, h), value[:, low * TILE : high * TILE], 1, 1)
        weights.append((grads * mask).astype(jnp.bfloat16))
    high, low = read_states(states_ref)
    outer = dot(grad_attn, high, 1, 1) + dot(grad_attn, low, 1, 1)
    grad_query = times_heads(weights, key_ref[...], 1) + outer * over_features(cols_ref[...], 0, BLOCK)
    grad_query_ref[...] = grad_query.astype(jnp.bfloat16)
    part_key_ref[...] = times_heads(weights, query_ref[...], 0)
    part_value_ref[...] = times_heads([probs_ref[h] for h in range(HEADS)], grad_attn, 0)
    attended = attention_ref[...] * inv_ref[:, 0:1] * row_of(gain_ref)
    attended_ref[...] = attended.astype(jnp.bfloat16)
    ready_ref[...] = jnp.zeros(ready_ref.shape, jnp.float32)


def last_kernel(
    scale, states_ref, cols_ref, key_ref, value_ref, part_key_ref, part_value_ref,
    grad_key_ref, grad_value_ref, grad_gain_ref,
):
    high, low = read_states(states_ref)
    tail = over_features(cols_ref[...], 4, BLOCK)
    key, value = key_ref[...], value_ref[...]
    outer = dot(value, high, 1, 1) + dot(value, low, 1, 1)
    grad_key_ref[...] = (part_key_ref[...] + outer * tail).astype(jnp.bfloat16)
    outer = dot(key, high) + dot(key, low)
    grad_value_ref[...] = (part_value_ref[...] + outer * tail).astype(jnp.bfloat16)
    count = states_ref.shape[0]
    gain = jnp.concatenate([states_ref[k] for k in range(count)], axis=0)
    grad_gain_ref[...] = (jnp.transpose(gain)[GAIN : GAIN + 1] * scale).reshape(gain.shape[0])


def reach_owners(pieces, backward):
    group, sub, lanes = pieces.shape
    pieces = exchange(pieces, "near", NEAR_ORDER)
    (total,) = on_chip(
        functools.partial(total_kernel, backward),
        [pltpu.VMEM((lax.axis_size("wide"), sub, lanes), jnp.float32)],
        [pieces],
        "group_total",
    )
    groups = exchange(total, "wide", wide_order(backward))
    inside = on_chip(
        functools.partial(local_prefix_kernel, backward),
        [pltpu.VMEM(pieces.shape, jnp.float32), pltpu.VMEM(pieces.shape, jnp.float32)],
        [pieces],
        "local_prefix",
        flops=8 * pieces.size,
    )
    return (*inside, groups)


def leave_owners(local_states, factors, groups, ready, backward):
    (states,) = on_chip(
        functools.partial(prefix_kernel, backward),
        [pltpu.VMEM(local_states.shape, jnp.float32)],
        [local_states, factors, groups, ready],
        "group_prefix",
    )
    return exchange(states, "near", NEAR_ORDER)


def local(queries, key_rows, values, log_decay, segment_ids, norm_gain, grad_out):
    tokens, features = queries.shape
    group = lax.axis_size("near")
    dp_count = lax.axis_size("wide") * group
    fsdp = lax.axis_size("fsdp")
    full = (tokens, features)
    mxu = 2 * tokens * tokens * HEAD * HEADS
    pieces, rows, cols = on_chip(
        summary_kernel,
        [
            pltpu.VMEM((group, SUB, TILE), jnp.float32),
            pltpu.VMEM((8, tokens), jnp.float32),
            pltpu.VMEM((tokens, 16), jnp.float32),
        ],
        [segment_ids, log_decay, key_rows, values],
        "summary",
        flops=mxu,
        held_in=pltpu.HBM,
    )
    scan = reach_owners(pieces, False)
    ready_shape = pltpu.VMEM((8, TILE), jnp.float32)
    probs, inner, ready = on_chip(
        inside_kernel,
        [
            pltpu.VMEM((HEADS, tokens, tokens), jnp.bfloat16),
            pltpu.VMEM(full, jnp.float32),
            ready_shape,
        ],
        [rows, cols, queries, key_rows, values],
        "inside",
        flops=4 * mxu,
        exps=HEADS * tokens * tokens,
    )
    state_in = leave_owners(*scan, ready, False)
    attention, sums = on_chip(
        attention_kernel,
        [pltpu.VMEM(full, jnp.float32), pltpu.VMEM((fsdp, 2, tokens), jnp.float32)],
        [state_in, inner, cols, queries, grad_out, norm_gain],
        "attention",
        flops=2 * mxu,
    )
    sums = lax.all_to_all(sums, "fsdp", 0, 0, tiled=True)
    grad_attn, inv, back_pieces = on_chip(
        functools.partial(gradient_kernel, features * fsdp),
        [
            pltpu.VMEM(full, jnp.bfloat16),
            pltpu.VMEM((tokens, 8), jnp.float32),
            pltpu.VMEM((group, SUB, TILE), jnp.float32),
        ],
        [sums, attention, grad_out, norm_gain, rows, cols, queries],
        "gradient",
        flops=mxu,
    )
    back_scan = reach_owners(back_pieces, True)
    grad_queries, part_key, part_value, attended, back_ready = on_chip(
        inside_back_kernel,
        [
            jax.ShapeDtypeStruct(full, jnp.bfloat16),
            pltpu.VMEM(full, jnp.float32),
            pltpu.VMEM(full, jnp.float32),
            jax.ShapeDtypeStruct(full, jnp.bfloat16),
            ready_shape,
        ],
        [rows, cols, queries, key_rows, values, probs, grad_attn, state_in, attention, inv, norm_gain],
        "inside_back",
        flops=8 * mxu,
        exps=HEADS * tokens * tokens,
    )
    back_in = leave_owners(*back_scan, back_ready, True)
    grad_keys, grad_values, grad_gain = on_chip(
        functools.partial(last_kernel, float(tokens * dp_count) ** (-0.5)),
        [
            jax.ShapeDtypeStruct(full, jnp.bfloat16),
            jax.ShapeDtypeStruct(full, jnp.bfloat16),
            jax.ShapeDtypeStruct((features,), jnp.float32),
        ],
        [back_in, cols, key_rows, values, part_key, part_value],
        "last",
        flops=4 * mxu,
    )
    return (attended, grad_queries, grad_keys, grad_values, grad_gain)


def columns(ref, count):
    picked = [[ref[k, :, lane : lane + 1] for k in range(count)] for lane in (PASS, NEAR, FAR)]
    return picked


def total_kernel(backward, pieces_ref, out_ref):
    count, rows, lanes = pieces_ref.shape
    order = places(NEAR_ORDER, backward)
    passes, near, far = columns(pieces_ref, count)
    if backward:
        near, far = far, near
    lane = lax.broadcasted_iota(jnp.int32, (rows, lanes), 1)
    running = pieces_ref[order[0]]
    gain = running
    through = passes[order[0]]
    for before, k in zip(order[:-1], order[1:]):
        piece = pieces_ref[k]
        carried = passes[k] * (far[before] == near[k]).astype(jnp.float32)
        running = piece + carried * running
        through = through * carried
        gain = gain + piece
    first, last = order[0], order[-1]
    out = jnp.where(lane < PASS, running, gain)
    out = jnp.where(lane == PASS, through, out)
    out = jnp.where(lane == NEAR, near[first], out)
    out = jnp.where(lane == FAR, far[last], out)
    for g in range(out_ref.shape[0]):
        out_ref[g] = out


def local_prefix_kernel(backward, pieces_ref, local_ref, factor_ref):
    count, rows, lanes = pieces_ref.shape
    order = places(NEAR_ORDER, backward)
    passes, near, far = columns(pieces_ref, count)
    if backward:
        near, far = far, near
    state = jnp.zeros((rows, lanes), jnp.float32)
    factor = jnp.ones((rows, lanes), jnp.float32)
    local_ref[order[0]] = state
    factor_ref[order[0]] = factor
    for before, k in zip(order[:-1], order[1:]):
        joined = (far[before] == near[k]).astype(jnp.float32)
        carried = jnp.broadcast_to(passes[before] * joined, (rows, lanes))
        state = pieces_ref[before] * joined + carried * state
        factor = carried * factor
        local_ref[k] = state
        factor_ref[k] = factor


def prefix_kernel(backward, local_ref, factor_ref, groups_ref, ready_ref, out_ref):
    del ready_ref
    count, rows, lanes = local_ref.shape
    group_count = groups_ref.shape[0]
    mine = lax.axis_index("wide")
    lane = lax.broadcasted_iota(jnp.int32, (rows, lanes), 1)
    running = jnp.zeros((rows, lanes), jnp.float32)
    gain = jnp.zeros((rows, lanes), jnp.float32)
    entering = running
    order = places(wide_order(backward), backward)
    passes, near, far = columns(groups_ref, group_count)
    for at, g in enumerate(order):
        if at:
            running = running * (far[order[at - 1]] == near[g]).astype(jnp.float32)
        entering = jnp.where(mine == wide_order(backward)[g], running, entering)
        piece = groups_ref[g]
        running = piece + passes[g] * running
        gain = gain + piece
    states = [jnp.where(lane < PASS, local_ref[k] + factor_ref[k] * entering, gain) for k in range(count)]
    for k in range(count):
        out_ref[k] = states[k]


def solution(mesh):
    dp_count, fsdp_count = mesh.devices.shape
    near_count = 16
    fine = Mesh(
        mesh.devices.reshape(dp_count // near_count, near_count, fsdp_count),
        ("wide", "near", "fsdp"),
    )
    dp = ("wide", "near")
    return jax.shard_map(
        local,
        mesh=fine,
        in_specs=(
            P(dp, "fsdp"),
            P(dp, "fsdp"),
            P(dp, "fsdp"),
            P("fsdp", dp),
            P(dp),
            P("fsdp"),
            P(dp, "fsdp"),
        ),
        out_specs=(P(dp, "fsdp"), P(dp, "fsdp"), P(dp, "fsdp"), P(dp, "fsdp"), P("fsdp")),
        check_vma=False,
    )
```

```python
import functools

import jax
import jax.numpy as jnp
from jax import lax
from jax.experimental import pallas as pl
from jax.experimental.pallas import tpu as pltpu
from jax.sharding import Mesh
from jax.sharding import PartitionSpec as P

BLOCK = 256
EPSILON = 1e-06
PRECISE = lax.Precision.HIGHEST
PASS, NEAR, FAR, GAIN = 96, 97, 98, 99


HEADS, HEAD, TILE = 4, 96, 128
SUB = 24
NEAR_ORDER = (5, 6, 7, 8, 9, 10, 11, 12, 13, 14, 15, 0, 1, 2, 3, 4)
FORWARD_WIDE_ORDER = (5, 1, 6, 2, 7, 3, 0, 4)
BACKWARD_WIDE_ORDER = (4, 0, 5, 1, 6, 2, 7, 3)
STARTS = tuple(HEAD * h % TILE for h in range(HEADS))
WINDOWS = tuple((HEAD * h // TILE, (HEAD * h + HEAD - 1) // TILE + 1) for h in range(HEADS))


def exchange(x, axis, order):
    return lax.all_to_all(x, axis, 0, 0, axis_index_groups=[list(order)], tiled=True)


def wide_order(backward):
    return BACKWARD_WIDE_ORDER if backward else FORWARD_WIDE_ORDER


def places(order, backward):
    found = [order.index(k) for k in range(len(order))]
    return found[::-1] if backward else found


def on_chip(kernel, outs, operands, name, flops=0, exps=0, held_in=pltpu.VMEM):
    placed, specs, moved = [], [], 0
    for x in operands:
        placed.append(pltpu.with_memory_space_constraint(x, held_in))
        inside = pltpu.SMEM if x.dtype == jnp.int32 else pltpu.VMEM
        specs.append(pl.BlockSpec(memory_space=inside))
        moved += x.size * x.dtype.itemsize
    for out in outs:
        moved += out.size * out.dtype.itemsize if hasattr(out, "size") else 0
    return pl.pallas_call(
        kernel,
        out_shape=outs,
        in_specs=specs,
        out_specs=[pl.BlockSpec(memory_space=pltpu.VMEM) for _ in outs],
        cost_estimate=pl.CostEstimate(
            flops=flops, bytes_accessed=moved, transcendentals=exps
        ),
        compiler_params=pltpu.CompilerParams(vmem_limit_bytes=40 * 1024 * 1024),
        name=name,
    )(*placed)


def dot(a, b, over_a=1, over_b=0):
    return lax.dot_general(
        a, b, (((over_a,), (over_b,)), ((), ())), preferred_element_type=jnp.float32
    )


def row_of(ref):
    return ref[...].reshape(1, ref.shape[0])


def pick_heads(parts, tile, rows):
    lane = lax.broadcasted_iota(jnp.int32, (rows, TILE), 1) + tile * TILE
    inside = [h for h in range(HEADS) if WINDOWS[h][0] <= tile < WINDOWS[h][1]]
    out = parts[inside[-1]]
    for h in inside[:-1][::-1]:
        out = jnp.where(lane < HEAD * (h + 1), parts[h], out)
    return out


def over_features(cols, first, rows):
    spread = [jnp.broadcast_to(cols[:, first + h : first + h + 1], (rows, TILE)) for h in range(HEADS)]
    return jnp.concatenate([pick_heads(spread, c, rows) for c in range(3)], axis=1)


def only_head(x, h):
    low, high = WINDOWS[h]
    x = x[:, low * TILE : high * TILE]
    lane = lax.broadcasted_iota(jnp.int32, x.shape, 1) + low * TILE
    inside = jnp.logical_and(lane >= HEAD * h, lane < HEAD * (h + 1))
    return jnp.where(inside, x, jnp.zeros_like(x))


def write_pieces(left, right, rows_ref, gain, out_ref):
    full = dot(left, right, 0, 0)
    lane = lax.broadcasted_iota(jnp.int32, (HEAD, TILE), 1)
    last = BLOCK - 1
    same, near, far = (rows_ref[r : r + 1, last:] for r in (4, 5, 6))
    for h in range(HEADS):
        low, high = WINDOWS[h]
        tiles = [full[HEAD * h : HEAD * (h + 1), TILE * c : TILE * (c + 1)] for c in range(low, high)]
        state = tiles[0] if len(tiles) == 1 else jnp.where(lane >= STARTS[h], tiles[0], tiles[1])
        if STARTS[h]:
            state = pltpu.roll(state, TILE - STARTS[h], 1)
        through = jnp.exp(rows_ref[h : h + 1, last:]) * same
        state = jnp.where(lane < HEAD, state, through)
        state = jnp.where(lane == NEAR, near, state)
        state = jnp.where(lane == FAR, far, state)
        state = jnp.where(lane == GAIN, 0.0 if gain is None else gain[HEAD * h : HEAD * (h + 1)], state)
        for i in range(HEAD // SUB):
            out_ref[h * (HEAD // SUB) + i] = state[i * SUB : (i + 1) * SUB]


def read_states(pieces_ref):
    lane = lax.broadcasted_iota(jnp.int32, (HEAD, TILE), 1)
    zero = jnp.zeros((HEAD, TILE), jnp.float32)
    parts = HEAD // SUB
    bands = []
    for h in range(HEADS):
        state = jnp.concatenate([pieces_ref[h * parts + i] for i in range(parts)], axis=0)
        state = jnp.where(lane < HEAD, state, 0.0)
        if STARTS[h]:
            state = pltpu.roll(state, STARTS[h], 1)
        low, high = WINDOWS[h]
        tiles = [zero] * 3
        if high - low == 1:
            tiles[low] = state
        else:
            tiles[low] = jnp.where(lane >= STARTS[h], state, 0.0)
            tiles[low + 1] = jnp.where(lane >= STARTS[h], 0.0, state)
        bands.append(jnp.concatenate(tiles, axis=1))
    whole = jnp.concatenate(bands, axis=0)
    high = whole.astype(jnp.bfloat16)
    return high, (whole - high.astype(jnp.float32)).astype(jnp.bfloat16)


def summary_kernel(segment_ref, decay_ref, key_ref, value_ref, pieces_ref, rows_ref, cols_ref):
    near, far = segment_ref[0], segment_ref[BLOCK - 1]
    same = (near == far).astype(jnp.float32)
    earlier = lax.broadcasted_iota(jnp.int32, (BLOCK, BLOCK), 0) <= lax.broadcasted_iota(
        jnp.int32, (BLOCK, BLOCK), 1
    )
    decay = decay_ref[...]
    decay = jnp.concatenate([decay, decay], axis=0)
    cumulative = jnp.dot(
        decay, earlier.astype(jnp.float32), precision=PRECISE, preferred_element_type=jnp.float32
    )
    row = lax.broadcasted_iota(jnp.int32, (8, BLOCK), 0)
    first_half = lax.broadcasted_iota(jnp.int32, (8, BLOCK), 1) < BLOCK // 2
    last = cumulative[:, BLOCK - 1 :]
    in_near = jnp.where(first_half, 1.0, same)
    in_far = jnp.where(first_half, same, 1.0)
    decays = jnp.where(
        row < HEADS, jnp.exp(cumulative) * in_near, jnp.exp(last - cumulative) * in_far
    )
    tags = jnp.where(row == 4, same, jnp.where(row == 5, near.astype(jnp.float32), far.astype(jnp.float32)))
    rows_ref[...] = jnp.where(row < HEADS, cumulative, tags)
    cols = jnp.transpose(jnp.concatenate([decays, cumulative], axis=0))
    cols_ref[...] = cols
    keyed = key_ref[...].astype(jnp.float32) * over_features(cols, 4, BLOCK)
    write_pieces(keyed.astype(jnp.bfloat16), value_ref[...], rows_ref, None, pieces_ref)


def decay_masks(rows_ref, cols_ref):
    t = lax.broadcasted_iota(jnp.int32, (BLOCK, BLOCK), 0)
    s = lax.broadcasted_iota(jnp.int32, (BLOCK, BLOCK), 1)
    half = BLOCK // 2
    together = jnp.logical_or((t < half) == (s < half), rows_ref[4:5, :] > 0.5)
    allowed = jnp.logical_and(t >= s, together)
    for h in range(HEADS):
        gap = cols_ref[:, 8 + h : 9 + h] - rows_ref[h : h + 1, :]
        yield h, jnp.exp(jnp.where(allowed, gap, -1e30))


def times_heads(weights, x, over):
    tiles = []
    for c in range(3):
        column = x[:, c * TILE : (c + 1) * TILE]
        parts = [
            dot(weights[h], column, over, 0) if WINDOWS[h][0] <= c < WINDOWS[h][1] else None
            for h in range(HEADS)
        ]
        tiles.append(pick_heads(parts, c, BLOCK))
    return jnp.concatenate(tiles, axis=1)


def inside_kernel(rows_ref, cols_ref, query_ref, key_ref, value_ref, probs_ref, inner_ref, ready_ref):
    query, key = query_ref[...], key_ref[...]
    weights = []
    for h, mask in decay_masks(rows_ref, cols_ref):
        low, high = WINDOWS[h]
        scores = dot(only_head(query, h), key[:, low * TILE : high * TILE], 1, 1)
        weights.append((scores * mask).astype(jnp.bfloat16))
        probs_ref[h] = weights[h]
    inner_ref[...] = times_heads(weights, value_ref[...], 1)
    ready_ref[...] = jnp.zeros(ready_ref.shape, jnp.float32)


def attention_kernel(
    states_ref, inner_ref, cols_ref, query_ref, grad_ref, gain_ref, attention_ref, sums_ref
):
    high, low = read_states(states_ref)
    query = query_ref[...]
    outer = dot(query, high) + dot(query, low)
    attention = inner_ref[...] + outer * over_features(cols_ref[...], 0, BLOCK)
    attention_ref[...] = attention
    squares = attention * attention
    products = grad_ref[...].astype(jnp.float32) * row_of(gain_ref) * attention
    sums = []
    for x in (squares, products):
        x = x[:, :TILE] + x[:, TILE : 2 * TILE] + x[:, 2 * TILE :]
        sums.append(jnp.sum(jnp.transpose(x), axis=0, keepdims=True))
    sums = jnp.concatenate(sums, axis=0)
    for k in range(sums_ref.shape[0]):
        sums_ref[k] = sums


def gradient_kernel(
    width, sums_ref, attention_ref, grad_ref, gain_ref, rows_ref, cols_ref, query_ref,
    grad_attn_ref, inv_ref, pieces_ref,
):
    sums = sums_ref[0]
    for k in range(1, sums_ref.shape[0]):
        sums = sums + sums_ref[k]
    inv = lax.rsqrt(sums[0:1] / width + EPSILON)
    dots = sums[1:2] * inv / width
    row = lax.broadcasted_iota(jnp.int32, (8, BLOCK), 0)
    both = jnp.transpose(jnp.where(row == 0, inv, dots))
    inv_ref[...] = both
    inv, dots = both[:, 0:1], both[:, 1:2]
    normed = attention_ref[...] * inv
    grad = grad_ref[...].astype(jnp.float32)
    grad_attn = (inv * (grad * row_of(gain_ref) - normed * dots)).astype(jnp.bfloat16)
    grad_attn_ref[...] = grad_attn
    gain = jnp.sum(grad * normed, axis=0, keepdims=True)
    gain = jnp.transpose(jnp.broadcast_to(gain, (8, gain.shape[1])))
    queued = query_ref[...].astype(jnp.float32) * over_features(cols_ref[...], 0, BLOCK)
    write_pieces(queued.astype(jnp.bfloat16), grad_attn, rows_ref, gain[:, 0:1], pieces_ref)


def inside_back_kernel(
    rows_ref, cols_ref, query_ref, key_ref, value_ref, probs_ref, grad_attn_ref, states_ref,
    attention_ref, inv_ref, gain_ref,
    grad_query_ref, part_key_ref, part_value_ref, attended_ref, ready_ref,
):
    grad_attn, value = grad_attn_ref[...], value_ref[...]
    weights = []
    for h, mask in decay_masks(rows_ref, cols_ref):
        low, high = WINDOWS[h]
        grads = dot(only_head(grad_attn, h), value[:, low * TILE : high * TILE], 1, 1)
        weights.append((grads * mask).astype(jnp.bfloat16))
    high, low = read_states(states_ref)
    outer = dot(grad_attn, high, 1, 1) + dot(grad_attn, low, 1, 1)
    grad_query = times_heads(weights, key_ref[...], 1) + outer * over_features(cols_ref[...], 0, BLOCK)
    grad_query_ref[...] = grad_query.astype(jnp.bfloat16)
    part_key_ref[...] = times_heads(weights, query_ref[...], 0)
    part_value_ref[...] = times_heads([probs_ref[h] for h in range(HEADS)], grad_attn, 0)
    attended = attention_ref[...] * inv_ref[:, 0:1] * row_of(gain_ref)
    attended_ref[...] = attended.astype(jnp.bfloat16)
    ready_ref[...] = jnp.zeros(ready_ref.shape, jnp.float32)


def last_kernel(
    scale, states_ref, cols_ref, key_ref, value_ref, part_key_ref, part_value_ref,
    grad_key_ref, grad_value_ref, grad_gain_ref,
):
    high, low = read_states(states_ref)
    tail = over_features(cols_ref[...], 4, BLOCK)
    key, value = key_ref[...], value_ref[...]
    outer = dot(value, high, 1, 1) + dot(value, low, 1, 1)
    grad_key_ref[...] = (part_key_ref[...] + outer * tail).astype(jnp.bfloat16)
    outer = dot(key, high) + dot(key, low)
    grad_value_ref[...] = (part_value_ref[...] + outer * tail).astype(jnp.bfloat16)
    count = states_ref.shape[0]
    gain = jnp.concatenate([states_ref[k] for k in range(count)], axis=0)
    grad_gain_ref[...] = (jnp.transpose(gain)[GAIN : GAIN + 1] * scale).reshape(gain.shape[0])


def reach_owners(pieces, backward):
    group, sub, lanes = pieces.shape
    pieces = exchange(pieces, "near", NEAR_ORDER)
    (total,) = on_chip(
        functools.partial(total_kernel, backward),
        [pltpu.VMEM((lax.axis_size("wide"), sub, lanes), jnp.float32)],
        [pieces],
        "group_total",
    )
    groups = exchange(total, "wide", wide_order(backward))
    inside = on_chip(
        functools.partial(local_prefix_kernel, backward),
        [pltpu.VMEM(pieces.shape, jnp.float32), pltpu.VMEM(pieces.shape, jnp.float32)],
        [pieces],
        "local_prefix",
        flops=8 * pieces.size,
    )
    return (*inside, groups)


def leave_owners(local_states, factors, groups, ready, backward):
    (states,) = on_chip(
        functools.partial(prefix_kernel, backward),
        [pltpu.VMEM(local_states.shape, jnp.float32)],
        [local_states, factors, groups, ready],
        "group_prefix",
    )
    return exchange(states, "near", NEAR_ORDER)


def local(queries, key_rows, values, log_decay, segment_ids, norm_gain, grad_out):
    tokens, features = queries.shape
    group = lax.axis_size("near")
    dp_count = lax.axis_size("wide") * group
    fsdp = lax.axis_size("fsdp")
    full = (tokens, features)
    mxu = 2 * tokens * tokens * HEAD * HEADS
    pieces, rows, cols = on_chip(
        summary_kernel,
        [
            pltpu.VMEM((group, SUB, TILE), jnp.float32),
            pltpu.VMEM((8, tokens), jnp.float32),
            pltpu.VMEM((tokens, 16), jnp.float32),
        ],
        [segment_ids, log_decay, key_rows, values],
        "summary",
        flops=mxu,
        held_in=pltpu.HBM,
    )
    scan = reach_owners(pieces, False)
    ready_shape = pltpu.VMEM((8, TILE), jnp.float32)
    probs, inner, ready = on_chip(
        inside_kernel,
        [
            pltpu.VMEM((HEADS, tokens, tokens), jnp.bfloat16),
            pltpu.VMEM(full, jnp.float32),
            ready_shape,
        ],
        [rows, cols, queries, key_rows, values],
        "inside",
        flops=4 * mxu,
        exps=HEADS * tokens * tokens,
    )
    state_in = leave_owners(*scan, ready, False)
    attention, sums = on_chip(
        attention_kernel,
        [pltpu.VMEM(full, jnp.float32), pltpu.VMEM((fsdp, 2, tokens), jnp.float32)],
        [state_in, inner, cols, queries, grad_out, norm_gain],
        "attention",
        flops=2 * mxu,
    )
    sums = lax.all_to_all(sums, "fsdp", 0, 0, tiled=True)
    grad_attn, inv, back_pieces = on_chip(
        functools.partial(gradient_kernel, features * fsdp),
        [
            pltpu.VMEM(full, jnp.bfloat16),
            pltpu.VMEM((tokens, 8), jnp.float32),
            pltpu.VMEM((group, SUB, TILE), jnp.float32),
        ],
        [sums, attention, grad_out, norm_gain, rows, cols, queries],
        "gradient",
        flops=mxu,
    )
    back_scan = reach_owners(back_pieces, True)
    grad_queries, part_key, part_value, attended, back_ready = on_chip(
        inside_back_kernel,
        [
            jax.ShapeDtypeStruct(full, jnp.bfloat16),
            pltpu.VMEM(full, jnp.float32),
            pltpu.VMEM(full, jnp.float32),
            jax.ShapeDtypeStruct(full, jnp.bfloat16),
            ready_shape,
        ],
        [rows, cols, queries, key_rows, values, probs, grad_attn, state_in, attention, inv, norm_gain],
        "inside_back",
        flops=8 * mxu,
        exps=HEADS * tokens * tokens,
    )
    back_in = leave_owners(*back_scan, back_ready, True)
    grad_keys, grad_values, grad_gain = on_chip(
        functools.partial(last_kernel, float(tokens * dp_count) ** (-0.5)),
        [
            jax.ShapeDtypeStruct(full, jnp.bfloat16),
            jax.ShapeDtypeStruct(full, jnp.bfloat16),
            jax.ShapeDtypeStruct((features,), jnp.float32),
        ],
        [back_in, cols, key_rows, values, part_key, part_value],
        "last",
        flops=4 * mxu,
    )
    return (attended, grad_queries, grad_keys, grad_values, grad_gain)


def columns(ref, count):
    picked = [[ref[k, :, lane : lane + 1] for k in range(count)] for lane in (PASS, NEAR, FAR)]
    return picked


def total_kernel(backward, pieces_ref, out_ref):
    count, rows, lanes = pieces_ref.shape
    order = places(NEAR_ORDER, backward)
    passes, near, far = columns(pieces_ref, count)
    if backward:
        near, far = far, near
    lane = lax.broadcasted_iota(jnp.int32, (rows, lanes), 1)
    running = pieces_ref[order[0]]
    gain = running
    through = passes[order[0]]
    for before, k in zip(order[:-1], order[1:]):
        piece = pieces_ref[k]
        carried = passes[k] * (far[before] == near[k]).astype(jnp.float32)
        running = piece + carried * running
        through = through * carried
        gain = gain + piece
    first, last = order[0], order[-1]
    out = jnp.where(lane < PASS, running, gain)
    out = jnp.where(lane == PASS, through, out)
    out = jnp.where(lane == NEAR, near[first], out)
    out = jnp.where(lane == FAR, far[last], out)
    for g in range(out_ref.shape[0]):
        out_ref[g] = out


def local_prefix_kernel(backward, pieces_ref, local_ref, factor_ref):
    count, rows, lanes = pieces_ref.shape
    order = places(NEAR_ORDER, backward)
    passes, near, far = columns(pieces_ref, count)
    if backward:
        near, far = far, near
    state = jnp.zeros((rows, lanes), jnp.float32)
    factor = jnp.ones((rows, lanes), jnp.float32)
    local_ref[order[0]] = state
    factor_ref[order[0]] = factor
    for before, k in zip(order[:-1], order[1:]):
        joined = (far[before] == near[k]).astype(jnp.float32)
        carried = jnp.broadcast_to(passes[before] * joined, (rows, lanes))
        state = pieces_ref[before] * joined + carried * state
        factor = carried * factor
        local_ref[k] = state
        factor_ref[k] = factor


def prefix_kernel(backward, local_ref, factor_ref, groups_ref, ready_ref, out_ref):
    del ready_ref
    count, rows, lanes = local_ref.shape
    group_count = groups_ref.shape[0]
    mine = lax.axis_index("wide")
    lane = lax.broadcasted_iota(jnp.int32, (rows, lanes), 1)
    running = jnp.zeros((rows, lanes), jnp.float32)
    gain = jnp.zeros((rows, lanes), jnp.float32)
    entering = running
    order = places(wide_order(backward), backward)
    passes, near, far = columns(groups_ref, group_count)
    for at, g in enumerate(order):
        if at:
            running = running * (far[order[at - 1]] == near[g]).astype(jnp.float32)
        entering = jnp.where(mine == wide_order(backward)[g], running, entering)
        piece = groups_ref[g]
        running = piece + passes[g] * running
        gain = gain + piece
    states = [jnp.where(lane < PASS, local_ref[k] + factor_ref[k] * entering, gain) for k in range(count)]
    for k in range(count):
        out_ref[k] = states[k]


def solution(mesh):
    dp_count, fsdp_count = mesh.devices.shape
    near_count = 16
    fine = Mesh(
        mesh.devices.reshape(dp_count // near_count, near_count, fsdp_count),
        ("wide", "near", "fsdp"),
    )
    dp = ("wide", "near")
    return jax.shard_map(
        local,
        mesh=fine,
        in_specs=(
            P(dp, "fsdp"),
            P(dp, "fsdp"),
            P(dp, "fsdp"),
            P("fsdp", dp),
            P(dp),
            P("fsdp"),
            P(dp, "fsdp"),
        ),
        out_specs=(P(dp, "fsdp"), P(dp, "fsdp"), P(dp, "fsdp"), P(dp, "fsdp"), P("fsdp")),
        check_vma=False,
    )
```
